128 devices in a mesh: fsdp: 16 (over x, z_hi, core), tp: 8 (over z_lo, y).
Axes of the slice: x: 4, y: 4, z: 4 (z_hi: 2, z_lo: 2; z = z_hi * 2 + z_lo), core: 2. Of those that a mesh axis runs over, the one named last changes fastest.
Arguments:
- activations: bfloat16 [8192, 5120], P('fsdp'), may hold values from -80 to 80
- cotangent: bfloat16 [8192, 5120], P('fsdp'), may hold values from -80 to 80
- lengths: int32 [32], P('fsdp'), may hold values from 64 to 256, as said below
- grow_operator: bfloat16 [5120, 4096], P('fsdp', 'tp'), may hold values from -0.078125 to 0.078125
- proxy_weight: bfloat16 [4096, 4096], P('fsdp', 'tp'), may hold values from -0.09375 to 0.09375
Outputs:
- update: bfloat16 [5120, 4096], P('fsdp', 'tp')
The draws below stay inside these ranges and needn't reach their ends.
Inputs may be any that keep to these rules, and one draw needn't show every extreme that they name: `lengths`: each entry is the length of one sequence; at least one is 256 and at least one is 64.
All inputs are finite; a program needn't handle non-finite values.
Results may differ from the reference program's by a relative error of at most 0.0057.
Values may be sent and summed in bfloat16 or wider, within the bound.
A program may use at most 128 MiB of HBM per device.

```python
import jax
import jax.numpy as jnp
from jax import lax

D = 5120
PD = 4096
LEN = 256
SEQS = 2
TOKENS = 8192
N_FSDP = 16


def column_scale(key, width):
    ramp = jnp.arange(width, dtype=jnp.float32) / width
    rough = jax.random.uniform(key, (width,), jnp.float32)
    return 10.0 ** (0.5 * ramp + 0.5 * rough)


def scaled_rows(key, rows_total, width):
    keys = jax.random.split(key, 2)
    scale = column_scale(keys[0], width)
    values = jnp.clip(jax.random.normal(keys[1], (rows_total, width), jnp.float32), -4.0, 4.0)
    return jnp.clip(values * scale[None, :], -80.0, 80.0)


def draw_activations(key, part):
    return scaled_rows(jax.random.fold_in(key, 11), TOKENS, D).astype(jnp.bfloat16)


def draw_cotangent(key, part):
    return scaled_rows(jax.random.fold_in(key, 23), TOKENS, D).astype(jnp.bfloat16)


def draw_lengths(key, part):
    drawn = jax.random.randint(jax.random.fold_in(key, 37), (SEQS * N_FSDP,), LEN // 4, LEN + 1, dtype=jnp.int32)
    return drawn.at[0].set(LEN).at[1].set(LEN // 4)


def shard_levels(rng, extent, pieces, least, top_value):
    def one(position, shards_of):
        heights = jax.random.uniform(jax.random.fold_in(jax.random.fold_in(rng, 6), position), (shards_of,), jnp.float32, least / len(pieces), top_value / len(pieces))
        return jnp.repeat(jnp.exp(heights), extent[position] // shards_of).reshape((-1,) + (1,) * (len(extent) - position - 1))

    gain = one(*pieces[0])
    for cut in pieces[1:]:
        gain = gain * one(*cut)
    return gain


def bell_draw(own_key, shape, scale, most, cuts=(), kind=jnp.bfloat16):
    values = jax.random.normal(own_key, shape, jnp.float32) * scale
    if len(cuts) > 0:
        values = shard_levels(own_key, shape, cuts, -0.22, 0.18) * values
    return jnp.clip(values, min=-most, max=most).astype(kind)


def setup_inputs(seed: int = 0) -> dict:
    splits = jax.random.split(jax.random.key(seed), 6)
    activations = draw_activations(jax.random.fold_in(splits[5], 71), 0)
    cotangent = draw_cotangent(jax.random.fold_in(splits[5], 71), 0)
    lengths = draw_lengths(jax.random.fold_in(splits[5], 71), 0)
    grow_operator = bell_draw(splits[3], (D, PD), D ** -0.5, 0.078125, ((0, 16), (1, 8)))
    proxy_weight = bell_draw(splits[4], (PD, PD), PD ** -0.5, 0.09375, ((0, 16), (1, 8)))
    return {"activations": activations, "cotangent": cotangent, "lengths": lengths, "grow_operator": grow_operator, "proxy_weight": proxy_weight}


def contract_tokens(left, right):
    return lax.dot_general(left, right, (((0,), (0,)), ((), ())), preferred_element_type=jnp.float32)

def contract_last(left, right):
    return lax.dot_general(left, right, (((1,), (1,)), ((), ())), preferred_element_type=jnp.float32)

def reference(activations, cotangent, lengths, grow_operator, proxy_weight):
    keep_mask = (jnp.arange(LEN, dtype=jnp.int32)[None, :] < lengths[:, None]).reshape(-1)
    grad_rows = jnp.where(keep_mask[:, None], cotangent, jnp.zeros_like(cotangent))
    forward = jnp.dot(activations, grow_operator, preferred_element_type=jnp.float32).astype(jnp.bfloat16)
    proxy_out = contract_last(forward, proxy_weight).astype(jnp.bfloat16)
    back = jnp.dot(grad_rows, grow_operator, preferred_element_type=jnp.float32).astype(jnp.bfloat16)
    delta = jnp.dot(back, proxy_weight, preferred_element_type=jnp.float32).astype(jnp.bfloat16)
    grad = contract_tokens(activations, delta) + contract_tokens(grad_rows, proxy_out)
    mean_sq = jnp.mean(grad * grad)
    return (grad * lax.rsqrt(mean_sq + 1e-06)).astype(jnp.bfloat16)
```

```python
import jax
import jax.numpy as jnp
from jax import lax
from jax.experimental import pallas as pl
from jax.experimental.pallas import tpu as pltpu
from jax.sharding import PartitionSpec as P

MESH = pl.DeviceIdType.MESH
F32, BF16 = jnp.float32, jnp.bfloat16

D = 5120
PD = 4096
LEN = 256
ROWS = 512
WR = 320
VR = 256
CT = 512
NC = 2
CW = CT // NC
NX = 4
NY = 4

G_Z, G_XP, G_XM, G_FP, G_FM, G_S, G_N = 0, 1, 3, 5, 6, 7, 15
T_Z, T_YP, T_YM, T_FP, T_FM, T_N = 0, 1, 3, 5, 6, 7
R_PF, R_PD, R_MF, R_MD, R_P2, R_M2, R_Z, R_C, R_N = 0, 1, 2, 3, 4, 5, 6, 7, 8
K_W = 0
K_V = K_W + NC * G_N
K_B = K_V + G_N
K_P = K_B + NC * T_N
K_G = K_P + NC * R_N
K_S = K_G + NC * R_N
K_N = K_S + 10


def dot(a, b):
    return jnp.dot(a, b, preferred_element_type=F32)


def dot_t(a, b):
    return lax.dot_general(a, b, (((1,), (1,)), ((), ())), preferred_element_type=F32)


def kernel(
    a_hbm, g_hbm, w_hbm, v_hbm, len_ref, out_ref,
    av, gv, at, gt, w0, w1, vg, bg, fw, dl, pp, ps, pr1, pr2, prz, gsib, gcore, gown, gs, gr1, gr2, grz,
    acc, sc, local, ss, rs,
):
    f = lax.axis_index("fsdp")
    t = lax.axis_index("tp")
    x, zh, core = f // 4, (f // 2) % 2, f % 2
    zl, y = t // 4, t % 4

    def fid(dx, r, other_core=0):
        c = core if other_core == 0 else 1 - core
        z = zh if r == 0 else 1 - zh
        return ((x + dx) % NX) * 4 + z * 2 + c

    def tid(dy, r):
        z = zl if r == 0 else 1 - zl
        return z * NY + (y + dy) % NY

    z_dev, sib = (fid(0, 1), t), (fid(0, 0, 1), t)
    xp, xm, x2 = (fid(1, 0), t), (fid(3, 0), t), (fid(2, 0), t)
    zl_dev = (f, tid(0, 1))
    yp, ym, y2 = (f, tid(1, 0)), (f, tid(3, 0)), (f, tid(2, 0))
    zd_dev = (fid(0, 1), tid(0, 1))
    peers = (z_dev, sib, xp, xm, x2, zl_dev, yp, ym, y2, zd_dev)

    load_a = pltpu.make_async_copy(a_hbm, av, local.at[0])
    load_g = pltpu.make_async_copy(g_hbm, gv, local.at[1])
    load_a.start()
    load_g.start()
    wg = (w0, w1)

    def wrows(src):
        return pl.ds(pl.multiple_of(src * WR, 64), WR)

    def vrows(src):
        return pl.ds(pl.multiple_of(src * VR, VR), VR)

    load_w = []
    for c in range(NC):
        load_w.append(
            pltpu.make_async_copy(w_hbm.at[:, pl.ds(c * CW, CW)], wg[c].at[wrows(f)], local.at[2 + c])
        )
    load_w.append(pltpu.make_async_copy(v_hbm, vg.at[vrows(f)], local.at[2 + NC]))
    for load in load_w:
        load.start()

    barrier = pltpu.get_barrier_semaphore()
    for peer in peers:
        pl.semaphore_signal(barrier, inc=1, device_id=peer, device_id_type=MESH)
    pl.semaphore_wait(barrier, len(peers))

    sent = []

    def remote(src, dst, k, dev):
        return pltpu.make_async_remote_copy(
            src_ref=src, dst_ref=dst, send_sem=ss.at[k], recv_sem=rs.at[k], device_id=dev, device_id_type=MESH
        )

    def send(src, dst, k, dev):
        copy = remote(src, dst, k, dev)
        copy.start()
        sent.append(copy)

    def arrived(dst, k):
        remote(dst, dst, k, sib).wait_recv()

    class Gather:
        def __init__(self, own, place, k):
            self.own, self.place, self.k = own, place, k

        def start(self):
            own, dst, k = self.own, self.place(f), self.k
            send(own, dst, k + G_Z, z_dev)
            send(own, dst, k + G_XP, xp)
            send(own, dst, k + G_XM, xm)
            send(own, dst, k + G_S, sib)

        def take_z(self):
            ref, k = self.place(fid(0, 1)), self.k
            arrived(ref, k + G_Z)
            send(ref, ref, k + G_XP + 1, xp)
            send(ref, ref, k + G_XM + 1, xm)
            send(ref, ref, k + G_S + 1, sib)

        def take_x(self, r):
            k = self.k
            back_ref, ahead_ref = self.place(fid(3, r)), self.place(fid(1, r))
            arrived(back_ref, k + G_XP + r)
            if r == 0:
                send(back_ref, back_ref, k + G_FP, xp)
            send(back_ref, back_ref, k + G_S + 6 + r, sib)
            arrived(ahead_ref, k + G_XM + r)
            if r == 1:
                send(ahead_ref, ahead_ref, k + G_FM, xm)
            send(ahead_ref, ahead_ref, k + G_S + 2 + r, sib)

        def take_far(self, r):
            k = self.k
            ref = self.place(fid(2, r))
            arrived(ref, k + (G_FP if r == 0 else G_FM))
            send(ref, ref, k + G_S + 4 + r, sib)

        def take_sib(self):
            for dx in range(NX):
                for r in range(2):
                    arrived(self.place(fid(dx, r, 1)), self.k + G_S + 2 * dx + r)

    def w_place(c):
        return lambda src: wg[c].at[wrows(src)]

    gw = [Gather(w_hbm.at[:, pl.ds(c * CW, CW)], w_place(c), K_W + c * G_N) for c in range(NC)]
    gvv = Gather(v_hbm, lambda src: vg.at[vrows(src)], K_V)

    def turn(src, dst, first, count):
        @pl.loop(first, first + count)
        def _(j):
            at_col = pl.multiple_of(j * 128, 128)
            dst[pl.ds(at_col, 128), :] = src[:, pl.ds(at_col, 128)].T

    gw[0].start()
    gw[1].start()
    load_a.wait()
    turn(av, at, 0, 20)
    gw[0].take_z()
    turn(av, at, 20, 20)
    gw[0].take_x(0)
    gw[1].take_z()
    gvv.start()
    load_g.wait()
    turn(gv, gt, 0, 20)
    gw[0].take_x(1)
    gw[1].take_x(0)
    turn(gv, gt, 20, 20)
    gw[0].take_far(0)
    gw[0].take_far(1)
    gvv.take_z()
    for load in load_w:
        load.wait()
    gw[0].take_sib()

    row_of = lax.broadcasted_iota(jnp.int32, (LEN, CW), 0)

    def keep(j, block):
        return jnp.where(row_of < len_ref[j], block, jnp.zeros_like(block))

    own_col = pl.multiple_of(t * CT, CT)

    def bcols(src, c):
        return bg.at[:, pl.ds(pl.multiple_of(src * CT + c * CW, CW), CW)]

    def project(c):
        @pl.loop(0, ROWS // LEN)
        def _(j):
            r0 = pl.ds(pl.multiple_of(j * LEN, LEN), LEN)
            block = dot(gv[r0, :], wg[c][...]).astype(BF16)
            bg[r0, pl.ds(pl.multiple_of(own_col + c * CW, CW), CW)] = keep(j, block)

        own = bcols(t, c)
        k = K_B + c * T_N
        send(own, own, k + T_Z, zl_dev)
        send(own, own, k + T_YP, yp)
        send(own, own, k + T_YM, ym)

        @pl.loop(0, ROWS // LEN)
        def _(j):
            r0 = pl.ds(pl.multiple_of(j * LEN, LEN), LEN)
            fw[r0, c * CW : (c + 1) * CW] = dot(av[r0, :], wg[c][...]).astype(BF16)

    def back_z(c):
        ref, k = bcols(tid(0, 1), c), K_B + c * T_N
        arrived(ref, k + T_Z)
        send(ref, ref, k + T_YP + 1, yp)
        send(ref, ref, k + T_YM + 1, ym)

    def back_y(c):
        k = K_B + c * T_N
        ref = bcols(tid(3, 0), c)
        arrived(ref, k + T_YP)
        send(ref, ref, k + T_FP, yp)
        ref = bcols(tid(1, 1), c)
        arrived(ref, k + T_YM + 1)
        send(ref, ref, k + T_FM, ym)

    def back_end(c):
        k = K_B + c * T_N
        arrived(bcols(tid(1, 0), c), k + T_YM)
        arrived(bcols(tid(3, 1), c), k + T_YP + 1)
        arrived(bcols(tid(2, 0), c), k + T_FP)
        arrived(bcols(tid(2, 1), c), k + T_FM)

    project(0)
    gw[1].take_x(1)
    gw[1].take_far(0)
    gw[1].take_far(1)
    gvv.take_x(0)
    back_z(0)
    gw[1].take_sib()
    project(1)
    gvv.take_x(1)
    back_y(0)
    gvv.take_far(0)
    gvv.take_far(1)
    back_z(1)
    gvv.take_sib()

    def partial_out(s):
        @pl.loop(0, 2 * NY)
        def _(i):
            dy, r = (i // 2 + 2) % NY, i % 2
            dest = ((zl + r) % 2) * NY + (y + dy) % NY
            rows = pl.ds(pl.multiple_of(dest * CT + s * CW, CW), CW)
            ps[s, 2 * dy + r] = dot_t(fw[...], vg[rows, :]).astype(BF16)

    class Sum:
        def __init__(self, blocks, near, far, zbuf, k, plus, minus, across):
            self.blocks, self.near, self.far, self.zbuf, self.k = blocks, near, far, zbuf, k
            self.plus, self.minus, self.across = plus, minus, across

        def start(self):
            k = self.k
            send(self.blocks.at[4], self.near.at[0], k + R_PF, self.plus)
            send(self.blocks.at[5], self.near.at[1], k + R_MF, self.minus)
            send(self.blocks.at[3], self.far.at[0], k + R_PD, self.plus)
            send(self.blocks.at[6], self.far.at[1], k + R_MD, self.minus)

        def middle(self):
            k = self.k
            for mine, slot, far, sem, out, dev in (
                (2, 0, 2, R_PF, R_P2, self.plus),
                (7, 1, 3, R_MF, R_M2, self.minus),
            ):
                arrived(self.near.at[slot], k + sem)
                self.blocks[mine] = (self.blocks[mine].astype(F32) + self.near[slot].astype(F32)).astype(BF16)
                send(self.blocks.at[mine], self.far.at[far], k + out, dev)

        def end(self, own, other):
            k = self.k
            arrived(self.far.at[0], k + R_PD)
            arrived(self.far.at[3], k + R_M2)
            self.blocks[1] = (other() + self.far[0].astype(F32) + self.far[3].astype(F32)).astype(BF16)
            send(self.blocks.at[1], self.zbuf, k + R_Z, self.across)
            arrived(self.far.at[1], k + R_MD)
            arrived(self.far.at[2], k + R_P2)
            acc[0 : own.shape[0], :] = own[...].astype(F32) + self.far[1].astype(F32) + self.far[2].astype(F32)

        def last(self, rows):
            arrived(self.zbuf, self.k + R_Z)
            return acc[0:rows, :] + self.zbuf[...].astype(F32)

    psum = [
        Sum(ps.at[s], pr1.at[s], pr2.at[s], prz.at[s], K_P + s * R_N, yp, ym, zl_dev) for s in range(NC)
    ]
    gsum = [
        Sum(gs.at[s], gr1.at[s], gr2.at[s], grz.at[s], K_G + s * R_N, xp, xm, z_dev) for s in range(NC)
    ]

    def finish_out(s):
        total = psum[s].last(ROWS).astype(BF16)
        for j in range(ROWS // LEN):
            pp[j * LEN : (j + 1) * LEN, s * CW : (s + 1) * CW] = keep(j, total[j * LEN : (j + 1) * LEN])

    def grad_block(i, s, c):
        dest = ((x + i // 2) % NX) * 4 + ((zh + i % 2) % 2) * 2 + c
        cols = slice(s * CW, (s + 1) * CW)
        return dot(at[wrows(dest), :], dl[:, cols]) + dot(gt[wrows(dest), :], pp[:, cols])

    def gradient(s):
        @pl.loop(0, 2 * NX)
        def _(i):
            gsib[s, i] = grad_block(i, s, 1 - core).astype(BF16)

        send(gsib.at[s], gcore.at[s], K_G + s * R_N + R_C, sib)

        @pl.loop(0, 2 * NX)
        def _(i):
            gown[i] = grad_block(i, s, core)

        arrived(gcore.at[s], K_G + s * R_N + R_C)

        @pl.loop(0, 2 * NX)
        def _(i):
            whole = gown[i] + gcore[s, i].astype(F32)
            gown[i] = whole
            gs[s, i] = whole.astype(BF16)

        gsum[s].start()

    partial_out(0)
    psum[0].start()
    partial_out(1)
    psum[1].start()
    back_y(1)
    back_end(0)
    back_end(1)
    psum[0].middle()
    for s in range(NC):
        cols = slice(s * CW, (s + 1) * CW)
        dl[:, cols] = dot(bg[...], vg[:, cols]).astype(BF16)
    psum[1].middle()
    psum[0].end(ps.at[0, 0], lambda: ps[0, 1].astype(F32))
    finish_out(0)
    gradient(0)
    psum[1].end(ps.at[1, 0], lambda: ps[1, 1].astype(F32))
    gsum[0].middle()
    finish_out(1)
    gsum[0].end(gown.at[0], lambda: gown[1])
    out0 = gsum[0].last(WR)
    res0 = out0
    sc_part = jnp.sum((out0 * out0).reshape(WR // 8, 8, CW), axis=0)
    gradient(1)
    gsum[1].middle()
    gsum[1].end(gown.at[0], lambda: gown[1])
    out1 = gsum[1].last(WR)
    sc_part = sc_part + jnp.sum((out1 * out1).reshape(WR // 8, 8, CW), axis=0)
    sc[0] = sc_part[:, 0:128] + sc_part[:, 128:256]

    send(sc.at[0], sc.at[1], K_S, sib)
    arrived(sc.at[1], K_S)
    sc[2] = sc[0] + sc[1]
    base, slot = 2, 1
    for devs in ((xp, xm, x2), (zl_dev, z_dev, zd_dev), (yp, ym, y2)):
        for j in range(3):
            send(sc.at[base], sc.at[base + 1 + j], K_S + slot + j, devs[j])
        for j in range(3):
            arrived(sc.at[base + 1 + j], K_S + slot + j)
        sc[base + 4] = (sc[base] + sc[base + 1]) + (sc[base + 2] + sc[base + 3])
        base, slot = base + 4, slot + 3
    scale = lax.rsqrt(jnp.sum(sc[base]) / (D * PD) + 1e-6)
    out_ref[:, 0:CW] = (res0 * scale).astype(BF16)
    out_ref[:, CW:CT] = (out1 * scale).astype(BF16)
    for copy in sent:
        copy.wait_send()


def per_device(activations, cotangent, lengths, grow_operator, proxy_weight):
    anywhere = pl.BlockSpec(memory_space=pl.ANY)
    return pl.pallas_call(
        kernel,
        out_shape=jax.ShapeDtypeStruct((WR, CT), BF16),
        in_specs=[anywhere] * 4 + [pl.BlockSpec(memory_space=pltpu.SMEM)],
        out_specs=pl.BlockSpec(memory_space=pltpu.VMEM),
        scratch_shapes=[
            pltpu.VMEM((ROWS, D), BF16),
            pltpu.VMEM((ROWS, D), BF16),
            pltpu.VMEM((D, ROWS), BF16),
            pltpu.VMEM((D, ROWS), BF16),
            pltpu.VMEM((D, CW), BF16),
            pltpu.VMEM((D, CW), BF16),
            pltpu.VMEM((PD, CT), BF16),
            pltpu.VMEM((ROWS, PD), BF16),
            pltpu.VMEM((ROWS, CT), BF16),
            pltpu.VMEM((ROWS, CT), BF16),
            pltpu.VMEM((ROWS, CT), BF16),
            pltpu.VMEM((NC, 2 * NY, ROWS, CW), BF16),
            pltpu.VMEM((NC, 2, ROWS, CW), BF16),
            pltpu.VMEM((NC, 4, ROWS, CW), BF16),
            pltpu.VMEM((NC, ROWS, CW), BF16),
            pltpu.VMEM((NC, 2 * NX, WR, CW), BF16),
            pltpu.VMEM((NC, 2 * NX, WR, CW), BF16),
            pltpu.VMEM((2 * NX, WR, CW), F32),
            pltpu.VMEM((NC, 2 * NX, WR, CW), BF16),
            pltpu.VMEM((NC, 2, WR, CW), BF16),
            pltpu.VMEM((NC, 4, WR, CW), BF16),
            pltpu.VMEM((NC, WR, CW), BF16),
            pltpu.VMEM((ROWS, CW), F32),
            pltpu.VMEM((15, 8, 128), F32),
            pltpu.SemaphoreType.DMA((3 + NC,)),
            pltpu.SemaphoreType.DMA((K_N,)),
            pltpu.SemaphoreType.DMA((K_N,)),
        ],
        compiler_params=pltpu.CompilerParams(
            collective_id=0, has_side_effects=True, vmem_limit_bytes=63 * 1024 * 1024
        ),
    )(activations, cotangent, grow_operator, proxy_weight, lengths)


def solution(mesh):
    placed = (P("fsdp", None), P("fsdp", None), P("fsdp"), P("fsdp", "tp"), P("fsdp", "tp"))
    return jax.shard_map(
        per_device, mesh=mesh, in_specs=placed, out_specs=P("fsdp", "tp"), check_vma=False
    )
```

```python
import jax
import jax.numpy as jnp
from jax import lax
from jax.experimental import pallas as pl
from jax.experimental.pallas import tpu as pltpu
from jax.sharding import PartitionSpec as P

MESH = pl.DeviceIdType.MESH
F32, BF16 = jnp.float32, jnp.bfloat16

D = 5120
PD = 4096
LEN = 256
ROWS = 512
WR = 320
VR = 256
CT = 512
NX = 4
NY = 4

WP = ((0, 128), (128, 128), (256, 256))
GP = ((0, 128), (128, 128), (256, 128), (384, 128))
ROUTE_B = "zzz"
ROUTE_P = "zyyz"
EARLY = (0, 1, 1, 1)
SEMS = 192

ORDER = (
    "w0.start", "w1.start", "w0.a0", "w0.b0", "w0.z", "ta0", "w1.a0", "w1.b0",
    "w1.z", "w2.start", "ta1", "ta2", "w0.a1", "w0.f0", "ta3", "w0.b1",
    "w1.a1", "tg0", "tg1", "w1.f0", "w2.z", "v.start", "tg2", "w1.b1",
    "w2.a0", "tg3", "w0.f1", "w0.sib", "b0.proj", "w1.f1", "w2.b0", "b0.fwd",
    "w1.sib", "b1.proj", "w2.a1", "w2.b1", "b1.fwd", "b0.yb", "b0.z", "v.z",
    "b1.yb", "b1.z", "v.a0", "v.b0", "b0.ya", "w2.f0", "w2.f1", "w2.sib",
    "b1.ya", "b2.proj", "b2.fwd", "b0.end", "v.a1", "v.b1", "b1.end", "b2.z",
    "v.f0", "v.f1", "b2.yb", "v.sib", "p0.part", "p1.part", "b2.ya", "p2.part",
    "p0.mm", "p3.part", "p0.mp", "b2.end", "delta", "p1.zm", "p0.eo", "p3.mp",
    "g1.pre", "p3.mm", "g2.pre", "p1.mm", "p1.mp", "g3.pre", "p2.zm", "p3.eo",
    "p1.last", "p0.last", "g0.sb", "g0.ow", "g0.comb", "g1.sb", "g1.ow", "g0.mm",
    "g0.mp", "p2.mm", "p2.mp", "p3.last", "g1.comb", "g0.eo", "p2.last", "g2.sb",
    "g0.last", "g1.mm", "g1.mp", "g2.ow", "g2.comb", "g3.sb", "g1.eo", "g3.ow",
    "g2.mm", "g2.mp", "g3.comb", "g1.last", "g2.eo", "g3.mm", "g3.mp", "g2.last",
    "g3.eo", "g3.last",
)


def dot(a, b):
    return jnp.dot(a, b, preferred_element_type=F32)


def dot_t(a, b):
    return lax.dot_general(a, b, (((1,), (1,)), ((), ())), preferred_element_type=F32)


def up(value):
    return value.astype(F32)


def kernel(a_hbm, g_hbm, w_hbm, v_hbm, len_ref, out_ref, *scratch):
    scratch = list(scratch)
    av, gv, at, gt, vg, bg, fw, dl, pp, res, sc, local, ss, rs = scratch[:14]
    del scratch[:14]

    def take(count):
        got = scratch[:count]
        del scratch[:count]
        return got

    wg = take(len(WP))
    ps, pnear, pfar, pz = (take(len(GP)) for _ in range(4))
    gsib, gcore, gown, gs, gnear, gfar, gz = (take(len(GP)) for _ in range(7))
    gpre = take(len(GP))

    f = lax.axis_index("fsdp")
    t = lax.axis_index("tp")
    x, zh, core = f // 4, (f // 2) % 2, f % 2
    zl, y = t // 4, t % 4

    def fid(dx, r, other_core=0):
        c = core if other_core == 0 else 1 - core
        z = zh if r == 0 else 1 - zh
        return ((x + dx) % NX) * 4 + z * 2 + c

    def tid(dy, r):
        z = zl if r == 0 else 1 - zl
        return z * NY + (y + dy) % NY

    z_dev, sib = (fid(0, 1), t), (fid(0, 0, 1), t)
    xp, xm, x2 = (fid(1, 0), t), (fid(3, 0), t), (fid(2, 0), t)
    xps, xms, x2s = (fid(1, 0, 1), t), (fid(3, 0, 1), t), (fid(2, 0, 1), t)
    zl_dev = (f, tid(0, 1))
    yp, ym, y2 = (f, tid(1, 0)), (f, tid(3, 0)), (f, tid(2, 0))
    zd_dev = (fid(0, 1), tid(0, 1))
    peers = (z_dev, sib, xp, xm, x2, xps, xms, x2s, zl_dev, yp, ym, y2, zd_dev)

    def wrows(src):
        return pl.ds(pl.multiple_of(src * WR, 64), WR)

    def vrows(src):
        return pl.ds(pl.multiple_of(src * VR, VR), VR)

    loads = [
        pltpu.make_async_copy(a_hbm, av, local.at[0]),
        pltpu.make_async_copy(g_hbm, gv, local.at[1]),
        pltpu.make_async_copy(v_hbm, vg.at[vrows(f)], local.at[2]),
    ]
    load_w = [
        pltpu.make_async_copy(w_hbm.at[:, pl.ds(first, width)], wg[c].at[wrows(f)], local.at[3 + c])
        for c, (first, width) in enumerate(WP)
    ]
    for load in loads + load_w:
        load.start()

    barrier = pltpu.get_barrier_semaphore()
    for peer in peers:
        pl.semaphore_signal(barrier, inc=1, device_id=peer, device_id_type=MESH)
    pl.semaphore_wait(barrier, len(peers))

    sent, sems, steps = [], {}, {}

    def remote(src, dst, key, dev):
        k = sems.setdefault(key, len(sems))
        return pltpu.make_async_remote_copy(
            src_ref=src, dst_ref=dst, send_sem=ss.at[k], recv_sem=rs.at[k], device_id=dev, device_id_type=MESH
        )

    def send(src, dst, key, dev):
        copy = remote(src, dst, key, dev)
        copy.start()
        sent.append(copy)

    def arrived(dst, key):
        remote(dst, dst, key, sib).wait_recv()

    def step(name, run, *args):
        steps[name] = lambda: run(*args)

    def turn(src, dst, quarter):
        if quarter == 0:
            loads[0 if src is av else 1].wait()
        part = D // 128 // 4

        @pl.loop(quarter * part, (quarter + 1) * part)
        def _(j):
            col = pl.multiple_of(j * 128, 128)
            dst[pl.ds(col, 128), :] = src[:, pl.ds(col, 128)].T

    for quarter in range(4):
        step(f"ta{quarter}", turn, av, at, quarter)
        step(f"tg{quarter}", turn, gv, gt, quarter)

    def gather(n, own, place, load):
        def start():
            dst = place(f)
            send(own, dst, (n, "z"), z_dev)
            send(own, dst, (n, "p", 0), xp)
            send(own, dst, (n, "m", 0), xm)
            send(own, dst, (n, "s", 0, 0), sib)

        def over_z():
            ref = place(fid(0, 1))
            arrived(ref, (n, "z"))
            send(ref, ref, (n, "p", 1), xp)
            send(ref, ref, (n, "m", 1), xm)
            send(ref, ref, (n, "s", 0, 1), sib)

        def behind(r):
            ref = place(fid(3, r))
            arrived(ref, (n, "p", r))
            if r == 0:
                send(ref, ref, (n, "f", 0), xp)
            send(ref, ref, (n, "s", 3, r), sib)

        def ahead(r):
            ref = place(fid(1, r))
            arrived(ref, (n, "m", r))
            if r == 1:
                send(ref, ref, (n, "f", 1), xm)
            send(ref, ref, (n, "s", 1, r), sib)

        def far(r):
            ref = place(fid(2, r))
            arrived(ref, (n, "f", r))
            send(ref, ref, (n, "s", 2, r), sib)

        def end():
            load.wait()
            for dx in range(NX):
                for r in range(2):
                    arrived(place(fid(dx, r, 1)), (n, "s", dx, r))

        step(f"{n}.start", start)
        step(f"{n}.z", over_z)
        for r in range(2):
            step(f"{n}.b{r}", behind, r)
            step(f"{n}.a{r}", ahead, r)
            step(f"{n}.f{r}", far, r)
        step(f"{n}.sib", end)

    def w_place(c):
        return lambda src: wg[c].at[wrows(src)]

    for c, (first, width) in enumerate(WP):
        gather(f"w{c}", w_hbm.at[:, pl.ds(first, width)], w_place(c), load_w[c])
    gather("v", v_hbm, lambda src: vg.at[vrows(src)], loads[2])

    def keep(j, block):
        row_of = lax.broadcasted_iota(jnp.int32, block.shape, 0)
        return jnp.where(row_of < len_ref[j], block, jnp.zeros_like(block))

    halves = (slice(0, LEN), slice(LEN, ROWS))

    def back(c):
        first, width = WP[c]
        n, route = f"b{c}", ROUTE_B[c]

        def cols(src):
            return pl.ds(pl.multiple_of(src * CT + first, 128), width)

        def block(dy, r):
            return bg.at[:, cols(tid(dy, r))]

        def half(dy, j):
            return bg.at[pl.ds(j * LEN, LEN), cols(tid(dy, 0))]

        def project():
            @pl.loop(0, ROWS // LEN)
            def _(j):
                r0 = pl.ds(pl.multiple_of(j * LEN, LEN), LEN)
                bg[r0, cols(t)] = keep(j, dot(gv[r0, :], wg[c][...]).astype(BF16))

            own = block(0, 0)
            if route == "z":
                send(own, own, (n, "z", 0), zl_dev)
            send(own, own, (n, "p", 0), yp)
            send(own, own, (n, "m", 0), ym)
            if route == "y":
                send(own, own, (n, "z", 0), zl_dev)

        def forward():
            @pl.loop(0, ROWS // LEN)
            def _(j):
                r0 = pl.ds(pl.multiple_of(j * LEN, LEN), LEN)
                fw[r0, first : first + width] = dot(av[r0, :], wg[c][...]).astype(BF16)

        def z_first():
            ref = block(0, 1)
            arrived(ref, (n, "z", 0))
            send(ref, ref, (n, "p", 1), yp)
            send(ref, ref, (n, "m", 1), ym)

        def behind():
            ref = block(3, 0)
            arrived(ref, (n, "p", 0))
            if route == "z":
                send(ref, ref, (n, "f", 0), yp)
            else:
                part = half(3, 0)
                send(part, part, (n, "f", 0), yp)
                send(ref, ref, (n, "z", 3), zl_dev)

        def ahead():
            if route == "z":
                ref = block(1, 1)
                arrived(ref, (n, "m", 1))
                send(ref, ref, (n, "f", 1), ym)
            else:
                ref, part = block(1, 0), half(1, 1)
                arrived(ref, (n, "m", 0))
                send(part, part, (n, "f", 1), ym)
                send(ref, ref, (n, "z", 1), zl_dev)

        def z_last():
            arrived(half(2, 0), (n, "f", 0))
            arrived(half(2, 1), (n, "f", 1))
            ref = block(2, 0)
            send(ref, ref, (n, "z", 2), zl_dev)

        def end():
            if route == "z":
                arrived(block(1, 0), (n, "m", 0))
                arrived(block(3, 1), (n, "p", 1))
                arrived(block(2, 0), (n, "f", 0))
                arrived(block(2, 1), (n, "f", 1))
            else:
                for dy in range(NY):
                    arrived(block(dy, 1), (n, "z", dy))

        step(f"{n}.proj", project)
        step(f"{n}.fwd", forward)
        step(f"{n}.z", z_first if route == "z" else z_last)
        step(f"{n}.yb", behind)
        step(f"{n}.ya", ahead)
        step(f"{n}.end", end)

    for c in range(len(WP)):
        back(c)

    def map_back():
        for first in range(0, CT, 256):
            dl[:, first : first + 256] = dot(bg[...], vg[:, first : first + 256]).astype(BF16)

    step("delta", map_back)

    def ring_sum(n, blocks, near, far, zbuf, plus, minus, across, own, other, finish):
        def start():
            send(blocks.at[4], near.at[0], (n, "pf"), plus)
            send(blocks.at[5], near.at[1], (n, "mf"), minus)
            send(blocks.at[3], far.at[0], (n, "pd"), plus)
            send(blocks.at[6], far.at[1], (n, "md"), minus)

        def through(mine, slot, key, to, out, dev):
            arrived(near.at[slot], (n, key))
            blocks[mine] = (up(blocks[mine]) + up(near[slot])).astype(BF16)
            send(blocks.at[mine], far.at[to], (n, out), dev)

        def end_other():
            arrived(far.at[0], (n, "pd"))
            arrived(far.at[3], (n, "m2"))
            blocks[1] = (up(other()) + up(far[0]) + up(far[3])).astype(BF16)
            send(blocks.at[1], zbuf, (n, "z"), across)

        def last():
            arrived(far.at[1], (n, "md"))
            arrived(far.at[2], (n, "p2"))
            arrived(zbuf, (n, "z"))
            finish((up(own()) + up(far[1])) + (up(far[2]) + up(zbuf[...])))

        step(f"{n}.mp", through, 2, 0, "pf", 2, "p2", plus)
        step(f"{n}.mm", through, 7, 1, "mf", 3, "m2", minus)
        step(f"{n}.eo", end_other)
        step(f"{n}.last", last)
        return start

    def cross_sum(n, blocks, near, far, zin, plus, minus, across, finish):
        def start():
            send(blocks.at[pl.ds(4, 4)], zin, (n, "z"), across)

        def whole(d, rows):
            return up(blocks[d, rows]) + up(zin[d, rows])

        def middle():
            arrived(zin, (n, "z"))
            for j, key, dev in ((0, "pf", plus), (1, "mf", minus)):
                blocks[2, halves[j]] = whole(2, halves[j]).astype(BF16)
                send(blocks.at[2, pl.ds(j * LEN, LEN)], near.at[j], (n, key), dev)

        def through(d, j, key, to, out, dev):
            arrived(near.at[j], (n, key))
            blocks[d, halves[j]] = (whole(d, halves[j]) + up(near[j])).astype(BF16)
            blocks[d, halves[1 - j]] = whole(d, halves[1 - j]).astype(BF16)
            send(blocks.at[d], far.at[to], (n, out), dev)

        def last():
            arrived(far.at[0], (n, "p2"))
            arrived(far.at[1], (n, "m2"))
            finish(whole(0, slice(0, ROWS)) + (up(far[0]) + up(far[1])))

        step(f"{n}.zm", middle)
        step(f"{n}.mp", through, 1, 0, "pf", 0, "p2", plus)
        step(f"{n}.mm", through, 3, 1, "mf", 1, "m2", minus)
        step(f"{n}.last", last)
        return start

    def proxy(s):
        first, width = GP[s]
        n, ring_first = f"p{s}", ROUTE_P[s] == "z"

        def finish(total):
            total = total.astype(BF16)
            for j in range(ROWS // LEN):
                pp[halves[j], first : first + width] = keep(j, total[halves[j]])

        if ring_first:
            start = ring_sum(
                n, ps[s], pnear[s], pfar[s], pz[s], yp, ym, zl_dev, lambda: ps[s][0], lambda: ps[s][1], finish
            )
        else:
            start = cross_sum(n, ps[s], pnear[s], pfar[s], pz[s], yp, ym, zl_dev, finish)

        def partial():
            @pl.loop(0, 2 * NY)
            def _(i):
                dy, r = (i // 2, i % 2) if ring_first else (i % 4, i // 4)
                dest = ((zl + r) % 2) * NY + (y + dy) % NY
                rows = pl.ds(pl.multiple_of(dest * CT + first, 128), width)
                ps[s][i] = dot_t(fw[...], vg[rows, :]).astype(BF16)

            start()

        step(f"{n}.part", partial)

    def gradient(s):
        first, width = GP[s]
        n, cols = f"g{s}", slice(first, first + width)

        def rows(i, c):
            return wrows(((x + i // 2) % NX) * 4 + ((zh + i % 2) % 2) * 2 + c)

        def early():
            @pl.loop(0, 2 * NX)
            def _(i):
                gpre[s][i] = dot(at[rows(i, 1 - core), :], dl[:, cols])
                gown[s][i] = dot(at[rows(i, core), :], dl[:, cols])

        def term(i, c, had):
            of_out = dot(gt[rows(i, c), :], pp[:, cols])
            if EARLY[s]:
                return had[i] + of_out
            return dot(at[rows(i, c), :], dl[:, cols]) + of_out

        def for_sibling():
            @pl.loop(0, 2 * NX)
            def _(i):
                gsib[s][i] = term(i, 1 - core, gpre[s]).astype(BF16)

            send(gsib[s], gcore[s], (n, "c"), sib)

        def for_own():
            @pl.loop(0, 2 * NX)
            def _(i):
                gown[s][i] = term(i, core, gown[s])

        def finish(total):
            res[:, cols] = total
            square = jnp.sum((total * total).reshape(WR // 8, 8, width), axis=0)
            square = sum(square[:, k : k + 128] for k in range(0, width, 128))
            sc[0] = square if s == 0 else sc[0] + square

        start = ring_sum(
            n, gs[s], gnear[s], gfar[s], gz[s], xp, xm, z_dev, lambda: gown[s][0], lambda: gown[s][1], finish
        )

        def combine():
            arrived(gcore[s], (n, "c"))

            @pl.loop(0, 2 * NX)
            def _(i):
                whole = gown[s][i] + up(gcore[s][i])
                gown[s][i] = whole
                gs[s][i] = whole.astype(BF16)

            start()

        if EARLY[s]:
            step(f"{n}.pre", early)
        step(f"{n}.sb", for_sibling)
        step(f"{n}.ow", for_own)
        step(f"{n}.comb", combine)

    for s in range(len(GP)):
        proxy(s)
        gradient(s)

    for name in ORDER:
        steps.pop(name)()
    assert not steps

    base = 0
    for devs in ((sib, xp, xm, x2, xps, xms, x2s), (zl_dev, z_dev, zd_dev), (yp, ym, y2)):
        for j, dev in enumerate(devs):
            send(sc.at[base], sc.at[base + 1 + j], ("q", base, j), dev)
        total = sc[base]
        for j in range(len(devs)):
            arrived(sc.at[base + 1 + j], ("q", base, j))
            total = total + sc[base + 1 + j]
        base = base + 1 + len(devs)
        sc[base] = total
    scale = lax.rsqrt(jnp.sum(sc[base]) / (D * PD) + 1e-6)
    out_ref[...] = (res[...] * scale).astype(BF16)
    for copy in sent:
        copy.wait_send()
    assert len(sems) <= SEMS


def per_device(activations, cotangent, lengths, grow_operator, proxy_weight):
    anywhere = pl.BlockSpec(memory_space=pl.ANY)

    def for_pieces(rows, shapes, kind=BF16):
        return [pltpu.VMEM(shape + (rows, width), kind) for (_, width), shape in zip(GP, shapes)]

    def same(*shape):
        return [shape] * len(GP)

    def routed(ring, cross):
        return [ring if route == "z" else cross for route in ROUTE_P]

    near = [
        pltpu.VMEM((2, ROWS if route == "z" else LEN, width), BF16) for (_, width), route in zip(GP, ROUTE_P)
    ]
    pre = [
        pltpu.VMEM((2 * NX, WR, width) if early else (8, 128), F32) for (_, width), early in zip(GP, EARLY)
    ]
    return pl.pallas_call(
        kernel,
        out_shape=jax.ShapeDtypeStruct((WR, CT), BF16),
        in_specs=[anywhere] * 4 + [pl.BlockSpec(memory_space=pltpu.SMEM)],
        out_specs=pl.BlockSpec(memory_space=pltpu.VMEM),
        scratch_shapes=[
            pltpu.VMEM((ROWS, D), BF16),
            pltpu.VMEM((ROWS, D), BF16),
            pltpu.VMEM((D, ROWS), BF16),
            pltpu.VMEM((D, ROWS), BF16),
            pltpu.VMEM((PD, CT), BF16),
            pltpu.VMEM((ROWS, PD), BF16),
            pltpu.VMEM((ROWS, CT), BF16),
            pltpu.VMEM((ROWS, CT), BF16),
            pltpu.VMEM((ROWS, CT), BF16),
            pltpu.VMEM((WR, CT), F32),
            pltpu.VMEM((17, 8, 128), F32),
            pltpu.SemaphoreType.DMA((3 + len(WP),)),
            pltpu.SemaphoreType.DMA((SEMS,)),
            pltpu.SemaphoreType.DMA((SEMS,)),
        ]
        + [pltpu.VMEM((D, width), BF16) for _, width in WP]
        + for_pieces(ROWS, same(2 * NY))
        + near
        + for_pieces(ROWS, routed((4,), (2,)))
        + for_pieces(ROWS, routed((), (4,)))
        + for_pieces(WR, same(2 * NX))
        + for_pieces(WR, same(2 * NX))
        + for_pieces(WR, same(2 * NX), F32)
        + for_pieces(WR, same(2 * NX))
        + for_pieces(WR, same(2))
        + for_pieces(WR, same(4))
        + for_pieces(WR, same())
        + pre,
        compiler_params=pltpu.CompilerParams(
            collective_id=0, has_side_effects=True, vmem_limit_bytes=63 * 1024 * 1024
        ),
    )(activations, cotangent, grow_operator, proxy_weight, lengths)


def solution(mesh):
    placed = (P("fsdp", None), P("fsdp", None), P("fsdp"), P("fsdp", "tp"), P("fsdp", "tp"))
    return jax.shard_map(
        per_device, mesh=mesh, in_specs=placed, out_specs=P("fsdp", "tp"), check_vma=False
    )
```

```python
import jax
import jax.numpy as jnp
from jax import lax
from jax.experimental import pallas as pl
from jax.experimental.pallas import tpu as pltpu
from jax.sharding import PartitionSpec as P

MESH = pl.DeviceIdType.MESH
F32, BF16 = jnp.float32, jnp.bfloat16

D = 5120
PD = 4096
LEN = 256
ROWS = 512
WR = 320
VR = 256
CT = 512
NX = 4
NY = 4

WP = ((0, 128), (128, 128), (256, 256))
GP = ((0, 128), (128, 128), (256, 128), (384, 128))
ROUTE_B = "zzy"
ROUTE_P = "zzzz"
EARLY = (1, 1, 1, 1)
SEMS = 192

ORDER = (
    "w0.start", "w1.start", "ta0", "w0.a0", "w0.b0", "w0.z", "ta1", "w1.a0",
    "w1.b0", "w1.z", "w2.start", "ta2", "ta3", "w0.f0", "w0.a1", "tg0",
    "w0.b1", "w1.a1", "tg1", "w1.f0", "tg2", "tg3", "w2.z", "v0.start",
    "w1.b1", "w2.a0", "w0.f1", "w0.sib", "b0.proj", "w2.b0", "b0.fwd", "w1.f1",
    "w2.b1", "w2.a1", "w1.sib", "b1.proj", "v0.z", "b1.fwd", "b0.yb", "b0.z",
    "v0.b0", "v0.a0", "b1.yb", "b1.z", "w2.f0", "w2.f1", "b0.ya", "w2.sib",
    "b2.proj", "b2.fwd", "b1.ya", "v0.b1", "v0.a1", "b0.end", "v0.f0", "b2.ya",
    "v0.f1", "b2.yb", "b1.end", "v0.sib", "p0.part", "p0.go", "p1.part", "b2.z",
    "p2.part", "p0.mm", "p3.part", "p0.mp", "p1.go", "p0.eo", "p1.mm", "b2.end",
    "delta", "p1.mp", "p2.go", "pre0", "p1.eo", "p0.last", "g0.sb", "p2.mm",
    "g0.ow", "g0.comb", "p2.mp", "p3.go", "p1.last", "g1.sb", "p2.eo", "g1.ow",
    "g0.mm", "g0.mp", "g1.comb", "p3.mm", "pre1", "p3.mp", "p2.last", "g0.eo",
    "g2.sb", "p3.eo", "g2.ow", "g2.comb", "g1.mm", "g0.last", "g1.mp", "p3.last",
    "g3.sb", "g2.mm", "g3.ow", "g3.comb", "g1.eo", "g2.mp", "g2.eo", "g3.mm",
    "g3.mp", "g1.last", "g2.last", "g3.eo", "g3.last",
)
VMEM_BYTES = 63 * 1024 * 1024


def dot(a, b):
    return jnp.dot(a, b, preferred_element_type=F32)


def dot_t(a, b):
    return lax.dot_general(a, b, (((1,), (1,)), ((), ())), preferred_element_type=F32)


def up(value):
    return value.astype(F32)


def kernel(a_hbm, g_hbm, w_hbm, v_hbm, len_ref, out_ref, *scratch):
    scratch = list(scratch)
    av, gv, at, gt, vg, bg, fw, dl, pp, sc, local, ss, rs = scratch[:13]
    del scratch[:13]

    def take(count):
        got = scratch[:count]
        del scratch[:count]
        return got

    wg = take(len(WP))
    ps, pnear, pfar, pz = (take(len(GP)) for _ in range(4))
    gsib, gcore, gown, gs, gnear, gfar, gz = (take(len(GP)) for _ in range(7))
    gpre = take(len(GP))

    f = lax.axis_index("fsdp")
    t = lax.axis_index("tp")
    x, zh, core = f // 4, (f // 2) % 2, f % 2
    zl, y = t // 4, t % 4

    def fid(dx, r, other_core=0):
        c = core if other_core == 0 else 1 - core
        z = zh if r == 0 else 1 - zh
        return ((x + dx) % NX) * 4 + z * 2 + c

    def tid(dy, r):
        z = zl if r == 0 else 1 - zl
        return z * NY + (y + dy) % NY

    z_dev, sib = (fid(0, 1), t), (fid(0, 0, 1), t)
    xp, xm, x2 = (fid(1, 0), t), (fid(3, 0), t), (fid(2, 0), t)
    xps, xms, x2s = (fid(1, 0, 1), t), (fid(3, 0, 1), t), (fid(2, 0, 1), t)
    zl_dev = (f, tid(0, 1))
    yp, ym, y2 = (f, tid(1, 0)), (f, tid(3, 0)), (f, tid(2, 0))
    zd_dev = (fid(0, 1), tid(0, 1))
    peers = (z_dev, sib, xp, xm, x2, xps, xms, x2s, zl_dev, yp, ym, y2, zd_dev)

    def wrows(src):
        return pl.ds(pl.multiple_of(src * WR, 64), WR)

    def vrows(src):
        return pl.ds(pl.multiple_of(src * VR, VR), VR)

    loads = [
        pltpu.make_async_copy(a_hbm, av, local.at[0]),
        pltpu.make_async_copy(g_hbm, gv, local.at[1]),
        pltpu.make_async_copy(v_hbm, vg.at[vrows(f)], local.at[2]),
    ]
    load_w = [
        pltpu.make_async_copy(w_hbm.at[:, pl.ds(first, width)], wg[c].at[wrows(f)], local.at[3 + c])
        for c, (first, width) in enumerate(WP)
    ]
    for load in loads + load_w:
        load.start()

    barrier = pltpu.get_barrier_semaphore()
    for peer in peers:
        pl.semaphore_signal(barrier, inc=1, device_id=peer, device_id_type=MESH)
    pl.semaphore_wait(barrier, len(peers))

    sent, sems, steps = [], {}, {}

    def remote(src, dst, key, dev):
        k = sems.setdefault(key, len(sems))
        return pltpu.make_async_remote_copy(
            src_ref=src, dst_ref=dst, send_sem=ss.at[k], recv_sem=rs.at[k], device_id=dev, device_id_type=MESH
        )

    def send(src, dst, key, dev):
        copy = remote(src, dst, key, dev)
        copy.start()
        sent.append(copy)

    def arrived(dst, key):
        remote(dst, dst, key, sib).wait_recv()

    def step(name, run, *args):
        steps[name] = lambda: run(*args)

    def turn(src, dst, quarter):
        if quarter == 0:
            loads[0 if src is av else 1].wait()
        part = D // 128 // 4

        @pl.loop(quarter * part, (quarter + 1) * part)
        def _(j):
            col = pl.multiple_of(j * 128, 128)
            dst[pl.ds(col, 128), :] = src[:, pl.ds(col, 128)].T

    for quarter in range(4):
        step(f"ta{quarter}", turn, av, at, quarter)
        step(f"tg{quarter}", turn, gv, gt, quarter)

    def gather(n, own, place, load):
        def start():
            dst = place(f)
            send(own, dst, (n, "z"), z_dev)
            send(own, dst, (n, "p", 0), xp)
            send(own, dst, (n, "m", 0), xm)
            send(own, dst, (n, "s", 0, 0), sib)

        def over_z():
            ref = place(fid(0, 1))
            arrived(ref, (n, "z"))
            send(ref, ref, (n, "p", 1), xp)
            send(ref, ref, (n, "m", 1), xm)
            send(ref, ref, (n, "s", 0, 1), sib)

        def behind(r):
            ref = place(fid(3, r))
            arrived(ref, (n, "p", r))
            if r == 0:
                send(ref, ref, (n, "f", 0), xp)
            send(ref, ref, (n, "s", 3, r), sib)

        def ahead(r):
            ref = place(fid(1, r))
            arrived(ref, (n, "m", r))
            if r == 1:
                send(ref, ref, (n, "f", 1), xm)
            send(ref, ref, (n, "s", 1, r), sib)

        def far(r):
            ref = place(fid(2, r))
            arrived(ref, (n, "f", r))
            send(ref, ref, (n, "s", 2, r), sib)

        def end():
            load.wait()
            for dx in range(NX):
                for r in range(2):
                    arrived(place(fid(dx, r, 1)), (n, "s", dx, r))

        step(f"{n}.start", start)
        step(f"{n}.z", over_z)
        for r in range(2):
            step(f"{n}.b{r}", behind, r)
            step(f"{n}.a{r}", ahead, r)
            step(f"{n}.f{r}", far, r)
        step(f"{n}.sib", end)

    def w_place(c):
        return lambda src: wg[c].at[wrows(src)]

    for c, (first, width) in enumerate(WP):
        gather(f"w{c}", w_hbm.at[:, pl.ds(first, width)], w_place(c), load_w[c])
    gather("v0", v_hbm, lambda src: vg.at[vrows(src)], loads[2])

    def keep(j, block):
        row_of = lax.broadcasted_iota(jnp.int32, block.shape, 0)
        return jnp.where(row_of < len_ref[j], block, jnp.zeros_like(block))

    halves = (slice(0, LEN), slice(LEN, ROWS))

    def back(c):
        first, width = WP[c]
        n, route = f"b{c}", ROUTE_B[c]

        def cols(src):
            return pl.ds(pl.multiple_of(src * CT + first, 128), width)

        def block(dy, r):
            return bg.at[:, cols(tid(dy, r))]

        def half(dy, j):
            return bg.at[pl.ds(j * LEN, LEN), cols(tid(dy, 0))]

        def project():
            @pl.loop(0, ROWS // LEN)
            def _(j):
                r0 = pl.ds(pl.multiple_of(j * LEN, LEN), LEN)
                bg[r0, cols(t)] = keep(j, dot(gv[r0, :], wg[c][...]).astype(BF16))

            own = block(0, 0)
            if route == "z":
                send(own, own, (n, "z", 0), zl_dev)
            send(own, own, (n, "p", 0), yp)
            send(own, own, (n, "m", 0), ym)
            if route == "y":
                send(own, own, (n, "z", 0), zl_dev)

        def forward():
            @pl.loop(0, ROWS // LEN)
            def _(j):
                r0 = pl.ds(pl.multiple_of(j * LEN, LEN), LEN)
                fw[r0, first : first + width] = dot(av[r0, :], wg[c][...]).astype(BF16)

        def z_first():
            ref = block(0, 1)
            arrived(ref, (n, "z", 0))
            send(ref, ref, (n, "p", 1), yp)
            send(ref, ref, (n, "m", 1), ym)

        def behind():
            ref = block(3, 0)
            arrived(ref, (n, "p", 0))
            if route == "z":
                send(ref, ref, (n, "f", 0), yp)
            else:
                part = half(3, 0)
                send(part, part, (n, "f", 0), yp)
                send(ref, ref, (n, "z", 3), zl_dev)

        def ahead():
            if route == "z":
                ref = block(1, 1)
                arrived(ref, (n, "m", 1))
                send(ref, ref, (n, "f", 1), ym)
            else:
                ref, part = block(1, 0), half(1, 1)
                arrived(ref, (n, "m", 0))
                send(part, part, (n, "f", 1), ym)
                send(ref, ref, (n, "z", 1), zl_dev)

        def z_last():
            arrived(half(2, 0), (n, "f", 0))
            arrived(half(2, 1), (n, "f", 1))
            ref = block(2, 0)
            send(ref, ref, (n, "z", 2), zl_dev)

        def end():
            if route == "z":
                arrived(block(1, 0), (n, "m", 0))
                arrived(block(3, 1), (n, "p", 1))
                arrived(block(2, 0), (n, "f", 0))
                arrived(block(2, 1), (n, "f", 1))
            else:
                for dy in range(NY):
                    arrived(block(dy, 1), (n, "z", dy))

        step(f"{n}.proj", project)
        step(f"{n}.fwd", forward)
        step(f"{n}.z", z_first if route == "z" else z_last)
        step(f"{n}.yb", behind)
        step(f"{n}.ya", ahead)
        step(f"{n}.end", end)

    for c in range(len(WP)):
        back(c)

    def map_back():
        for first in range(0, CT, 256):
            dl[:, first : first + 256] = dot(bg[...], vg[:, first : first + 256]).astype(BF16)

    step("delta", map_back)

    def ring_sum(n, blocks, near, far, zbuf, plus, minus, across, own, other, finish):
        def start():
            send(blocks.at[4], near.at[0], (n, "pf"), plus)
            send(blocks.at[5], near.at[1], (n, "mf"), minus)
            send(blocks.at[3], far.at[0], (n, "pd"), plus)
            send(blocks.at[6], far.at[1], (n, "md"), minus)

        def through(mine, slot, key, to, out, dev):
            arrived(near.at[slot], (n, key))
            blocks[mine] = (up(blocks[mine]) + up(near[slot])).astype(BF16)
            send(blocks.at[mine], far.at[to], (n, out), dev)

        def end_other():
            arrived(far.at[0], (n, "pd"))
            arrived(far.at[3], (n, "m2"))
            blocks[1] = (up(other()) + up(far[0]) + up(far[3])).astype(BF16)
            send(blocks.at[1], zbuf, (n, "z"), across)

        def last():
            arrived(far.at[1], (n, "md"))
            arrived(far.at[2], (n, "p2"))
            arrived(zbuf, (n, "z"))
            finish((up(own()) + up(far[1])) + (up(far[2]) + up(zbuf[...])))

        step(f"{n}.mp", through, 2, 0, "pf", 2, "p2", plus)
        step(f"{n}.mm", through, 7, 1, "mf", 3, "m2", minus)
        step(f"{n}.eo", end_other)
        step(f"{n}.last", last)
        return start

    def cross_sum(n, blocks, near, far, zin, plus, minus, across, finish):
        def start():
            send(blocks.at[pl.ds(4, 4)], zin, (n, "z"), across)

        def whole(d, rows):
            return up(blocks[d, rows]) + up(zin[d, rows])

        def middle():
            arrived(zin, (n, "z"))
            for j, key, dev in ((0, "pf", plus), (1, "mf", minus)):
                blocks[2, halves[j]] = whole(2, halves[j]).astype(BF16)
                send(blocks.at[2, pl.ds(j * LEN, LEN)], near.at[j], (n, key), dev)

        def through(d, j, key, to, out, dev):
            arrived(near.at[j], (n, key))
            blocks[d, halves[j]] = (whole(d, halves[j]) + up(near[j])).astype(BF16)
            blocks[d, halves[1 - j]] = whole(d, halves[1 - j]).astype(BF16)
            send(blocks.at[d], far.at[to], (n, out), dev)

        def last():
            arrived(far.at[0], (n, "p2"))
            arrived(far.at[1], (n, "m2"))
            finish(whole(0, slice(0, ROWS)) + (up(far[0]) + up(far[1])))

        step(f"{n}.zm", middle)
        step(f"{n}.mp", through, 1, 0, "pf", 0, "p2", plus)
        step(f"{n}.mm", through, 3, 1, "mf", 1, "m2", minus)
        step(f"{n}.last", last)
        return start

    def proxy(s):
        first, width = GP[s]
        n, ring_first = f"p{s}", ROUTE_P[s] == "z"

        def finish(total):
            total = total.astype(BF16)
            for j in range(ROWS // LEN):
                pp[halves[j], first : first + width] = keep(j, total[halves[j]])

        if ring_first:
            start = ring_sum(
                n, ps[s], pnear[s], pfar[s], pz[s], yp, ym, zl_dev, lambda: ps[s][0], lambda: ps[s][1], finish
            )
        else:
            start = cross_sum(n, ps[s], pnear[s], pfar[s], pz[s], yp, ym, zl_dev, finish)

        def partial():
            @pl.loop(0, 2 * NY)
            def _(i):
                dy, r = (i // 2, i % 2) if ring_first else (i % 4, i // 4)
                dest = ((zl + r) % 2) * NY + (y + dy) % NY
                rows = pl.ds(pl.multiple_of(dest * CT + first, 128), width)
                ps[s][i] = dot_t(fw[...], vg[rows, :]).astype(BF16)

        step(f"{n}.part", partial)
        step(f"{n}.go", start)

    def gradient(s):
        first, width = GP[s]
        n, cols = f"g{s}", slice(first, first + width)

        def rows(i, c):
            return wrows(((x + i // 2) % NX) * 4 + ((zh + i % 2) % 2) * 2 + c)

        def term(i, c, had):
            of_out = dot(gt[rows(i, c), :], pp[:, cols])
            if EARLY[s]:
                return had[i] + of_out
            return dot(at[rows(i, c), :], dl[:, cols]) + of_out

        def for_sibling():
            @pl.loop(0, 2 * NX)
            def _(i):
                gsib[s][i] = term(i, 1 - core, gpre[s]).astype(BF16)

            send(gsib[s], gcore[s], (n, "c"), sib)

        def for_own():
            @pl.loop(0, 2 * NX)
            def _(i):
                gown[s][i] = term(i, core, gown[s])

        def finish(total):
            gpre[s][0] = total
            square = jnp.sum((total * total).reshape(WR // 8, 8, width), axis=0)
            square = sum(square[:, k : k + 128] for k in range(0, width, 128))
            sc[0] = square if s == 0 else sc[0] + square

        start = ring_sum(
            n, gs[s], gnear[s], gfar[s], gz[s], xp, xm, z_dev, lambda: gown[s][0], lambda: gown[s][1], finish
        )

        def combine():
            arrived(gcore[s], (n, "c"))

            @pl.loop(0, 2 * NX)
            def _(i):
                whole = gown[s][i] + up(gcore[s][i])
                gown[s][i] = whole
                gs[s][i] = whole.astype(BF16)

            start()

        step(f"{n}.sb", for_sibling)
        step(f"{n}.ow", for_own)
        step(f"{n}.comb", combine)

    def delta_term(h):
        first = GP[2 * h][0]

        @pl.loop(0, 2 * NX)
        def _(i):
            base = ((x + i // 2) % NX) * 4 + ((zh + i % 2) % 2) * 2
            for c, to in ((1 - core, gpre), (core, gown)):
                both = dot(at[wrows(base + c), :], dl[:, first : first + 256])
                to[2 * h][i] = both[:, 0:128]
                to[2 * h + 1][i] = both[:, 128:256]

    for s in range(len(GP)):
        proxy(s)
        gradient(s)
    for h in range(len(GP) // 2):
        step(f"pre{h}", delta_term, h)

    for name in ORDER:
        steps.pop(name)()
    assert not steps

    base = 0
    for devs in ((sib, xp, xm, x2, xps, xms, x2s), (zl_dev, z_dev, zd_dev), (yp, ym, y2)):
        for j, dev in enumerate(devs):
            send(sc.at[base], sc.at[base + 1 + j], ("q", base, j), dev)
        total = sc[base]
        for j in range(len(devs)):
            arrived(sc.at[base + 1 + j], ("q", base, j))
            total = total + sc[base + 1 + j]
        base = base + 1 + len(devs)
        sc[base] = total
    scale = lax.rsqrt(jnp.sum(sc[base]) / (D * PD) + 1e-6)
    for s, (first, width) in enumerate(GP):
        out_ref[:, first : first + width] = (gpre[s][0] * scale).astype(BF16)
    for copy in sent:
        copy.wait_send()
    assert len(sems) <= SEMS


def per_device(activations, cotangent, lengths, grow_operator, proxy_weight):
    anywhere = pl.BlockSpec(memory_space=pl.ANY)

    def for_pieces(rows, shapes, kind=BF16):
        return [pltpu.VMEM(shape + (rows, width), kind) for (_, width), shape in zip(GP, shapes)]

    def same(*shape):
        return [shape] * len(GP)

    def routed(ring, cross):
        return [ring if route == "z" else cross for route in ROUTE_P]

    near = [
        pltpu.VMEM((2, ROWS if route == "z" else LEN, width), BF16) for (_, width), route in zip(GP, ROUTE_P)
    ]
    pre = [
        pltpu.VMEM((2 * NX, WR, width) if early else (8, 128), F32) for (_, width), early in zip(GP, EARLY)
    ]
    return pl.pallas_call(
        kernel,
        out_shape=jax.ShapeDtypeStruct((WR, CT), BF16),
        in_specs=[anywhere] * 4 + [pl.BlockSpec(memory_space=pltpu.SMEM)],
        out_specs=pl.BlockSpec(memory_space=pltpu.VMEM),
        scratch_shapes=[
            pltpu.VMEM((ROWS, D), BF16),
            pltpu.VMEM((ROWS, D), BF16),
            pltpu.VMEM((D, ROWS), BF16),
            pltpu.VMEM((D, ROWS), BF16),
            pltpu.VMEM((PD, CT), BF16),
            pltpu.VMEM((ROWS, PD), BF16),
            pltpu.VMEM((ROWS, CT), BF16),
            pltpu.VMEM((ROWS, CT), BF16),
            pltpu.VMEM((ROWS, CT), BF16),
            pltpu.VMEM((17, 8, 128), F32),
            pltpu.SemaphoreType.DMA((3 + len(WP),)),
            pltpu.SemaphoreType.DMA((SEMS,)),
            pltpu.SemaphoreType.DMA((SEMS,)),
        ]
        + [pltpu.VMEM((D, width), BF16) for _, width in WP]
        + for_pieces(ROWS, same(2 * NY))
        + near
        + for_pieces(ROWS, routed((4,), (2,)))
        + for_pieces(ROWS, routed((), (4,)))
        + for_pieces(WR, same(2 * NX))
        + for_pieces(WR, same(2 * NX))
        + for_pieces(WR, same(2 * NX), F32)
        + for_pieces(WR, same(2 * NX))
        + for_pieces(WR, same(2))
        + for_pieces(WR, same(4))
        + for_pieces(WR, same())
        + pre,
        compiler_params=pltpu.CompilerParams(
            collective_id=0, has_side_effects=True, vmem_limit_bytes=VMEM_BYTES
        ),
    )(activations, cotangent, grow_operator, proxy_weight, lengths)


def solution(mesh):
    placed = (P("fsdp", None), P("fsdp", None), P("fsdp"), P("fsdp", "tp"), P("fsdp", "tp"))
    return jax.shard_map(
        per_device, mesh=mesh, in_specs=placed, out_specs=P("fsdp", "tp"), check_vma=False
    )
```

```python
import jax
import jax.numpy as jnp
from jax import lax
from jax.experimental import pallas as pl
from jax.experimental.pallas import tpu as pltpu
from jax.sharding import PartitionSpec as P

MESH = pl.DeviceIdType.MESH
F32, BF16 = jnp.float32, jnp.bfloat16

D = 5120
PD = 4096
LEN = 256
ROWS = 512
WR = 320
VR = 256
CT = 512
NX = 4
NY = 4

WP = ((0, 128), (128, 128), (256, 256))
GP = ((0, 128), (128, 128), (256, 128), (384, 128))
ROUTE_B = "zzy"
ROUTE_P = "zzzz"
EARLY = (1, 1, 1, 1)
SEMS = 192

ORDER = (
    "w0.start", "w1.start", "ta0", "w0.a0", "w0.b0", "w0.z", "ta1", "w1.a0",
    "w1.b0", "w1.z", "w2.start", "ta2", "ta3", "w0.f0", "w0.a1", "tg0",
    "w0.b1", "w1.a1", "tg1", "w1.f0", "tg2", "tg3", "w2.z", "v0.start",
    "w1.b1", "w2.a0", "w0.f1", "w0.sib", "b0.proj", "w2.b0", "b0.fwd", "w1.f1",
    "w2.b1", "w2.a1", "w1.sib", "b1.proj", "v0.z", "b1.fwd", "b0.yb", "b0.z",
    "v0.b0", "v0.a0", "b1.yb", "b1.z", "w2.f0", "w2.f1", "b0.ya", "w2.sib",
    "b2.proj", "b2.fwd", "b1.ya", "v0.b1", "v0.a1", "b0.end", "v0.f0", "b2.ya",
    "v0.f1", "b2.yb", "b1.end", "v0.sib", "p0.part", "p0.go", "p1.part", "b2.z",
    "p2.part", "p0.mm", "p3.part", "p0.mp", "p1.go", "p0.eo", "p1.mm", "b2.end",
    "delta", "p1.mp", "p2.go", "pre0", "p1.eo", "p0.last", "g0.sb", "p2.mm",
    "g0.ow", "g0.comb", "p2.mp", "p3.go", "p1.last", "g1.sb", "p2.eo", "g1.ow",
    "g0.mm", "g0.mp", "g1.comb", "p3.mm", "pre1", "p3.mp", "p2.last", "g0.eo",
    "g2.sb", "p3.eo", "g2.ow", "g2.comb", "g1.mm", "g0.last", "g1.mp", "p3.last",
    "g3.sb", "g2.mm", "g3.ow", "g3.comb", "g1.eo", "g2.mp", "g2.eo", "g3.mm",
    "g3.mp", "g1.last", "g2.last", "g3.eo", "g3.last",
)
VMEM_BYTES = 63 * 1024 * 1024


def dot(a, b):
    return jnp.dot(a, b, preferred_element_type=F32)


def dot_t(a, b):
    return lax.dot_general(a, b, (((1,), (1,)), ((), ())), preferred_element_type=F32)


def up(value):
    return value.astype(F32)


def kernel(a_hbm, g_hbm, w_hbm, v_hbm, len_ref, out_ref, *scratch):
    scratch = list(scratch)
    av, gv, at, gt, vg, bg, fw, dl, pp, sc, local, ss, rs = scratch[:13]
    del scratch[:13]

    def take(count):
        got = scratch[:count]
        del scratch[:count]
        return got

    wg = take(len(WP))
    ps, pnear, pfar, pz = (take(len(GP)) for _ in range(4))
    gsib, gcore, gown, gs, gnear, gfar, gz = (take(len(GP)) for _ in range(7))
    gpre = take(len(GP))

    f = lax.axis_index("fsdp")
    t = lax.axis_index("tp")
    x, zh, core = f // 4, (f // 2) % 2, f % 2
    zl, y = t // 4, t % 4

    def fid(dx, r, other_core=0):
        c = core if other_core == 0 else 1 - core
        z = zh if r == 0 else 1 - zh
        return ((x + dx) % NX) * 4 + z * 2 + c

    def tid(dy, r):
        z = zl if r == 0 else 1 - zl
        return z * NY + (y + dy) % NY

    z_dev, sib = (fid(0, 1), t), (fid(0, 0, 1), t)
    xp, xm, x2 = (fid(1, 0), t), (fid(3, 0), t), (fid(2, 0), t)
    xps, xms, x2s = (fid(1, 0, 1), t), (fid(3, 0, 1), t), (fid(2, 0, 1), t)
    zl_dev = (f, tid(0, 1))
    yp, ym, y2 = (f, tid(1, 0)), (f, tid(3, 0)), (f, tid(2, 0))
    zd_dev = (fid(0, 1), tid(0, 1))
    peers = (z_dev, sib, xp, xm, x2, xps, xms, x2s, zl_dev, yp, ym, y2, zd_dev)

    def wrows(src):
        return pl.ds(pl.multiple_of(src * WR, 64), WR)

    def vrows(src):
        return pl.ds(pl.multiple_of(src * VR, VR), VR)

    loads = [
        pltpu.make_async_copy(a_hbm, av, local.at[0]),
        pltpu.make_async_copy(g_hbm, gv, local.at[1]),
        pltpu.make_async_copy(v_hbm, vg.at[vrows(f)], local.at[2]),
    ]
    load_w = [
        pltpu.make_async_copy(w_hbm.at[:, pl.ds(first, width)], wg[c].at[wrows(f)], local.at[3 + c])
        for c, (first, width) in enumerate(WP)
    ]
    for load in loads + load_w:
        load.start()

    barrier = pltpu.get_barrier_semaphore()
    for peer in peers:
        pl.semaphore_signal(barrier, inc=1, device_id=peer, device_id_type=MESH)
    pl.semaphore_wait(barrier, len(peers))

    sent, sems, steps = [], {}, {}

    def remote(src, dst, key, dev):
        k = sems.setdefault(key, len(sems))
        return pltpu.make_async_remote_copy(
            src_ref=src, dst_ref=dst, send_sem=ss.at[k], recv_sem=rs.at[k], device_id=dev, device_id_type=MESH
        )

    def send(src, dst, key, dev):
        copy = remote(src, dst, key, dev)
        copy.start()
        sent.append(copy)

    def arrived(dst, key):
        remote(dst, dst, key, sib).wait_recv()

    def step(name, run, *args):
        steps[name] = lambda: run(*args)

    def turn(src, dst, quarter):
        if quarter == 0:
            loads[0 if src is av else 1].wait()
        part = D // 128 // 4

        @pl.loop(quarter * part, (quarter + 1) * part, unroll=2)
        def _(j):
            col = pl.multiple_of(j * 128, 128)
            dst[pl.ds(col, 128), :] = src[:, pl.ds(col, 128)].T

    for quarter in range(4):
        step(f"ta{quarter}", turn, av, at, quarter)
        step(f"tg{quarter}", turn, gv, gt, quarter)

    def gather(n, own, place, load):
        def start():
            dst = place(f)
            send(own, dst, (n, "z"), z_dev)
            send(own, dst, (n, "p", 0), xp)
            send(own, dst, (n, "m", 0), xm)
            send(own, dst, (n, "s", 0, 0), sib)

        def over_z():
            ref = place(fid(0, 1))
            arrived(ref, (n, "z"))
            send(ref, ref, (n, "p", 1), xp)
            send(ref, ref, (n, "m", 1), xm)
            send(ref, ref, (n, "s", 0, 1), sib)

        def behind(r):
            ref = place(fid(3, r))
            arrived(ref, (n, "p", r))
            if r == 0:
                send(ref, ref, (n, "f", 0), xp)
            send(ref, ref, (n, "s", 3, r), sib)

        def ahead(r):
            ref = place(fid(1, r))
            arrived(ref, (n, "m", r))
            if r == 1:
                send(ref, ref, (n, "f", 1), xm)
            send(ref, ref, (n, "s", 1, r), sib)

        def far(r):
            ref = place(fid(2, r))
            arrived(ref, (n, "f", r))
            send(ref, ref, (n, "s", 2, r), sib)

        def end():
            load.wait()
            for dx in range(NX):
                for r in range(2):
                    arrived(place(fid(dx, r, 1)), (n, "s", dx, r))

        step(f"{n}.start", start)
        step(f"{n}.z", over_z)
        for r in range(2):
            step(f"{n}.b{r}", behind, r)
            step(f"{n}.a{r}", ahead, r)
            step(f"{n}.f{r}", far, r)
        step(f"{n}.sib", end)

    def w_place(c):
        return lambda src: wg[c].at[wrows(src)]

    for c, (first, width) in enumerate(WP):
        gather(f"w{c}", w_hbm.at[:, pl.ds(first, width)], w_place(c), load_w[c])
    gather("v0", v_hbm, lambda src: vg.at[vrows(src)], loads[2])

    def keep(j, block):
        row_of = lax.broadcasted_iota(jnp.int32, block.shape, 0)
        return jnp.where(row_of < len_ref[j], block, jnp.zeros_like(block))

    halves = (slice(0, LEN), slice(LEN, ROWS))

    def back(c):
        first, width = WP[c]
        n, route = f"b{c}", ROUTE_B[c]

        def cols(src):
            return pl.ds(pl.multiple_of(src * CT + first, 128), width)

        def block(dy, r):
            return bg.at[:, cols(tid(dy, r))]

        def half(dy, j):
            return bg.at[pl.ds(j * LEN, LEN), cols(tid(dy, 0))]

        def project():
            @pl.loop(0, ROWS // LEN, unroll=2)
            def _(j):
                r0 = pl.ds(pl.multiple_of(j * LEN, LEN), LEN)
                bg[r0, cols(t)] = keep(j, dot(gv[r0, :], wg[c][...]).astype(BF16))

            own = block(0, 0)
            if route == "z":
                send(own, own, (n, "z", 0), zl_dev)
            send(own, own, (n, "p", 0), yp)
            send(own, own, (n, "m", 0), ym)
            if route == "y":
                send(own, own, (n, "z", 0), zl_dev)

        def forward():
            @pl.loop(0, ROWS // LEN, unroll=2)
            def _(j):
                r0 = pl.ds(pl.multiple_of(j * LEN, LEN), LEN)
                fw[r0, first : first + width] = dot(av[r0, :], wg[c][...]).astype(BF16)

        def z_first():
            ref = block(0, 1)
            arrived(ref, (n, "z", 0))
            send(ref, ref, (n, "p", 1), yp)
            send(ref, ref, (n, "m", 1), ym)

        def behind():
            ref = block(3, 0)
            arrived(ref, (n, "p", 0))
            if route == "z":
                send(ref, ref, (n, "f", 0), yp)
            else:
                part = half(3, 0)
                send(part, part, (n, "f", 0), yp)
                send(ref, ref, (n, "z", 3), zl_dev)

        def ahead():
            if route == "z":
                ref = block(1, 1)
                arrived(ref, (n, "m", 1))
                send(ref, ref, (n, "f", 1), ym)
            else:
                ref, part = block(1, 0), half(1, 1)
                arrived(ref, (n, "m", 0))
                send(part, part, (n, "f", 1), ym)
                send(ref, ref, (n, "z", 1), zl_dev)

        def z_last():
            arrived(half(2, 0), (n, "f", 0))
            arrived(half(2, 1), (n, "f", 1))
            ref = block(2, 0)
            send(ref, ref, (n, "z", 2), zl_dev)

        def end():
            if route == "z":
                arrived(block(1, 0), (n, "m", 0))
                arrived(block(3, 1), (n, "p", 1))
                arrived(block(2, 0), (n, "f", 0))
                arrived(block(2, 1), (n, "f", 1))
            else:
                for dy in range(NY):
                    arrived(block(dy, 1), (n, "z", dy))

        step(f"{n}.proj", project)
        step(f"{n}.fwd", forward)
        step(f"{n}.z", z_first if route == "z" else z_last)
        step(f"{n}.yb", behind)
        step(f"{n}.ya", ahead)
        step(f"{n}.end", end)

    for c in range(len(WP)):
        back(c)

    def map_back():
        for first in range(0, CT, 256):
            dl[:, first : first + 256] = dot(bg[...], vg[:, first : first + 256]).astype(BF16)

    step("delta", map_back)

    def ring_sum(n, blocks, near, far, zbuf, plus, minus, across, own, other, finish):
        def start():
            send(blocks.at[4], near.at[0], (n, "pf"), plus)
            send(blocks.at[5], near.at[1], (n, "mf"), minus)
            send(blocks.at[3], far.at[0], (n, "pd"), plus)
            send(blocks.at[6], far.at[1], (n, "md"), minus)

        def through(mine, slot, key, to, out, dev):
            arrived(near.at[slot], (n, key))
            blocks[mine] = (up(blocks[mine]) + up(near[slot])).astype(BF16)
            send(blocks.at[mine], far.at[to], (n, out), dev)

        def end_other():
            arrived(far.at[0], (n, "pd"))
            arrived(far.at[3], (n, "m2"))
            blocks[1] = (up(other()) + up(far[0]) + up(far[3])).astype(BF16)
            send(blocks.at[1], zbuf, (n, "z"), across)

        def last():
            arrived(far.at[1], (n, "md"))
            arrived(far.at[2], (n, "p2"))
            arrived(zbuf, (n, "z"))
            finish((up(own()) + up(far[1])) + (up(far[2]) + up(zbuf[...])))

        step(f"{n}.mp", through, 2, 0, "pf", 2, "p2", plus)
        step(f"{n}.mm", through, 7, 1, "mf", 3, "m2", minus)
        step(f"{n}.eo", end_other)
        step(f"{n}.last", last)
        return start

    def cross_sum(n, blocks, near, far, zin, plus, minus, across, finish):
        def start():
            send(blocks.at[pl.ds(4, 4)], zin, (n, "z"), across)

        def whole(d, rows):
            return up(blocks[d, rows]) + up(zin[d, rows])

        def middle():
            arrived(zin, (n, "z"))
            for j, key, dev in ((0, "pf", plus), (1, "mf", minus)):
                blocks[2, halves[j]] = whole(2, halves[j]).astype(BF16)
                send(blocks.at[2, pl.ds(j * LEN, LEN)], near.at[j], (n, key), dev)

        def through(d, j, key, to, out, dev):
            arrived(near.at[j], (n, key))
            blocks[d, halves[j]] = (whole(d, halves[j]) + up(near[j])).astype(BF16)
            blocks[d, halves[1 - j]] = whole(d, halves[1 - j]).astype(BF16)
            send(blocks.at[d], far.at[to], (n, out), dev)

        def last():
            arrived(far.at[0], (n, "p2"))
            arrived(far.at[1], (n, "m2"))
            finish(whole(0, slice(0, ROWS)) + (up(far[0]) + up(far[1])))

        step(f"{n}.zm", middle)
        step(f"{n}.mp", through, 1, 0, "pf", 0, "p2", plus)
        step(f"{n}.mm", through, 3, 1, "mf", 1, "m2", minus)
        step(f"{n}.last", last)
        return start

    def proxy(s):
        first, width = GP[s]
        n, ring_first = f"p{s}", ROUTE_P[s] == "z"

        def finish(total):
            total = total.astype(BF16)
            for j in range(ROWS // LEN):
                pp[halves[j], first : first + width] = keep(j, total[halves[j]])

        if ring_first:
            start = ring_sum(
                n, ps[s], pnear[s], pfar[s], pz[s], yp, ym, zl_dev, lambda: ps[s][0], lambda: ps[s][1], finish
            )
        else:
            start = cross_sum(n, ps[s], pnear[s], pfar[s], pz[s], yp, ym, zl_dev, finish)

        def partial():
            @pl.loop(0, 2 * NY, unroll=4)
            def _(i):
                dy, r = (i // 2, i % 2) if ring_first else (i % 4, i // 4)
                dest = ((zl + r) % 2) * NY + (y + dy) % NY
                rows = pl.ds(pl.multiple_of(dest * CT + first, 128), width)
                ps[s][i] = dot_t(fw[...], vg[rows, :]).astype(BF16)

        step(f"{n}.part", partial)
        step(f"{n}.go", start)

    def gradient(s):
        first, width = GP[s]
        n, cols = f"g{s}", slice(first, first + width)

        def rows(i, c):
            return wrows(((x + i // 2) % NX) * 4 + ((zh + i % 2) % 2) * 2 + c)

        def term(i, c, had):
            of_out = dot(gt[rows(i, c), :], pp[:, cols])
            if EARLY[s]:
                return had[i] + of_out
            return dot(at[rows(i, c), :], dl[:, cols]) + of_out

        def for_sibling():
            @pl.loop(0, 2 * NX, unroll=4)
            def _(i):
                gsib[s][i] = term(i, 1 - core, gpre[s]).astype(BF16)

            send(gsib[s], gcore[s], (n, "c"), sib)

        def for_own():
            @pl.loop(0, 2 * NX, unroll=4)
            def _(i):
                gown[s][i] = term(i, core, gown[s])

        def finish(total):
            gpre[s][0] = total
            square = jnp.sum((total * total).reshape(WR // 8, 8, width), axis=0)
            square = sum(square[:, k : k + 128] for k in range(0, width, 128))
            sc[0] = square if s == 0 else sc[0] + square

        start = ring_sum(
            n, gs[s], gnear[s], gfar[s], gz[s], xp, xm, z_dev, lambda: gown[s][0], lambda: gown[s][1], finish
        )

        def combine():
            arrived(gcore[s], (n, "c"))

            @pl.loop(0, 2 * NX)
            def _(i):
                whole = gown[s][i] + up(gcore[s][i])
                gown[s][i] = whole
                gs[s][i] = whole.astype(BF16)

            start()

        step(f"{n}.sb", for_sibling)
        step(f"{n}.ow", for_own)
        step(f"{n}.comb", combine)

    def delta_term(h):
        first = GP[2 * h][0]

        @pl.loop(0, 2 * NX, unroll=2)
        def _(i):
            base = ((x + i // 2) % NX) * 4 + ((zh + i % 2) % 2) * 2
            for c, to in ((1 - core, gpre), (core, gown)):
                both = dot(at[wrows(base + c), :], dl[:, first : first + 256])
                to[2 * h][i] = both[:, 0:128]
                to[2 * h + 1][i] = both[:, 128:256]

    for s in range(len(GP)):
        proxy(s)
        gradient(s)
    for h in range(len(GP) // 2):
        step(f"pre{h}", delta_term, h)

    for name in ORDER:
        steps.pop(name)()
    assert not steps

    base = 0
    for devs in ((sib, xp, xm, x2, xps, xms, x2s), (zl_dev, z_dev, zd_dev), (yp, ym, y2)):
        for j, dev in enumerate(devs):
            send(sc.at[base], sc.at[base + 1 + j], ("q", base, j), dev)
        total = sc[base]
        for j in range(len(devs)):
            arrived(sc.at[base + 1 + j], ("q", base, j))
            total = total + sc[base + 1 + j]
        base = base + 1 + len(devs)
        sc[base] = total
    scale = lax.rsqrt(jnp.sum(sc[base]) / (D * PD) + 1e-6)
    for s, (first, width) in enumerate(GP):
        out_ref[:, first : first + width] = (gpre[s][0] * scale).astype(BF16)
    for copy in sent:
        copy.wait_send()
    assert len(sems) <= SEMS


def per_device(activations, cotangent, lengths, grow_operator, proxy_weight):
    anywhere = pl.BlockSpec(memory_space=pl.ANY)

    def for_pieces(rows, shapes, kind=BF16):
        return [pltpu.VMEM(shape + (rows, width), kind) for (_, width), shape in zip(GP, shapes)]

    def same(*shape):
        return [shape] * len(GP)

    def routed(ring, cross):
        return [ring if route == "z" else cross for route in ROUTE_P]

    near = [
        pltpu.VMEM((2, ROWS if route == "z" else LEN, width), BF16) for (_, width), route in zip(GP, ROUTE_P)
    ]
    pre = [
        pltpu.VMEM((2 * NX, WR, width) if early else (8, 128), F32) for (_, width), early in zip(GP, EARLY)
    ]
    return pl.pallas_call(
        kernel,
        out_shape=jax.ShapeDtypeStruct((WR, CT), BF16),
        in_specs=[anywhere] * 4 + [pl.BlockSpec(memory_space=pltpu.SMEM)],
        out_specs=pl.BlockSpec(memory_space=pltpu.VMEM),
        scratch_shapes=[
            pltpu.VMEM((ROWS, D), BF16),
            pltpu.VMEM((ROWS, D), BF16),
            pltpu.VMEM((D, ROWS), BF16),
            pltpu.VMEM((D, ROWS), BF16),
            pltpu.VMEM((PD, CT), BF16),
            pltpu.VMEM((ROWS, PD), BF16),
            pltpu.VMEM((ROWS, CT), BF16),
            pltpu.VMEM((ROWS, CT), BF16),
            pltpu.VMEM((ROWS, CT), BF16),
            pltpu.VMEM((17, 8, 128), F32),
            pltpu.SemaphoreType.DMA((3 + len(WP),)),
            pltpu.SemaphoreType.DMA((SEMS,)),
            pltpu.SemaphoreType.DMA((SEMS,)),
        ]
        + [pltpu.VMEM((D, width), BF16) for _, width in WP]
        + for_pieces(ROWS, same(2 * NY))
        + near
        + for_pieces(ROWS, routed((4,), (2,)))
        + for_pieces(ROWS, routed((), (4,)))
        + for_pieces(WR, same(2 * NX))
        + for_pieces(WR, same(2 * NX))
        + for_pieces(WR, same(2 * NX), F32)
        + for_pieces(WR, same(2 * NX))
        + for_pieces(WR, same(2))
        + for_pieces(WR, same(4))
        + for_pieces(WR, same())
        + pre,
        compiler_params=pltpu.CompilerParams(
            collective_id=0, has_side_effects=True, vmem_limit_bytes=VMEM_BYTES
        ),
    )(activations, cotangent, grow_operator, proxy_weight, lengths)


def solution(mesh):
    placed = (P("fsdp", None), P("fsdp", None), P("fsdp"), P("fsdp", "tp"), P("fsdp", "tp"))
    return jax.shard_map(
        per_device, mesh=mesh, in_specs=placed, out_specs=P("fsdp", "tp"), check_vma=False
    )
```

```python
import jax
import jax.numpy as jnp
from jax import lax
from jax.experimental import pallas as pl
from jax.experimental.pallas import tpu as pltpu
from jax.sharding import PartitionSpec as P

MESH = pl.DeviceIdType.MESH
F32, BF16 = jnp.float32, jnp.bfloat16

D = 5120
PD = 4096
LEN = 256
ROWS = 512
WR = 320
VR = 256
CT = 512
NX = 4
NY = 4

WP = ((0, 128), (128, 128), (256, 256))
GP = ((0, 128), (128, 128), (256, 128), (384, 128))
ROUTE_B = "zzy"
ROUTE_P = "zzzy"
EARLY = (1, 1, 1, 1)
SEMS = 192

ORDER = (
    "w0.start", "w2.start", "w0.z", "w1.start", "w2.z", "w0.b0", "ta0", "w2.b0",
    "w0.b1", "w1.z", "ta1", "ta2", "ta3", "w2.a0", "w0.a1", "tg0",
    "tg1", "w0.a0", "w2.a1", "tg2", "w2.b1", "w1.b0", "w1.a1", "w1.a0",
    "w0.f0", "v0.start", "w0.f1", "w0.sib", "w2.f0", "b0.proj", "w2.f1", "w2.sib",
    "b2.proj", "tg3", "w1.b1", "v0.z", "b0.fwd", "b0.z", "w1.f0", "w1.f1",
    "v0.a0", "w1.sib", "b1.proj", "b2.ya", "v0.b0", "b2.yb", "v0.b1", "v0.a1",
    "b1.z", "b0.yb", "b2.fwd", "b1.fwd", "b1.yb", "b2.z", "b0.ya", "v0.f0",
    "v0.f1", "v0.sib", "b1.ya", "p0.part", "p0.go", "b0.end", "p1.part", "p3.part",
    "p3.go", "p0.mm", "p0.mp", "p1.go", "b2.end", "b1.end", "delta", "p2.part",
    "pre0", "p1.mm", "p0.eo", "p1.mp", "p2.go", "pre1", "p1.eo", "p0.last",
    "g0.sb", "p2.mm", "p2.mp", "g0.ow", "g0.comb", "p3.zm", "p1.last", "g1.sb",
    "p2.eo", "g1.ow", "g1.comb", "p3.mp", "g0.mm", "p3.mm", "g0.mp", "p2.last",
    "g2.sb", "g1.mm", "g2.ow", "p3.last", "g2.comb", "g3.sb", "g3.ow", "g3.comb",
    "g0.eo", "g1.mp", "g2.mm", "g2.mp", "g3.mm", "g1.eo", "g2.eo", "g3.mp",
    "g3.eo", "g0.last", "g1.last", "g2.last", "g3.last",
)
VMEM_BYTES = 63 * 1024 * 1024


def dot(a, b):
    return jnp.dot(a, b, preferred_element_type=F32)


def dot_t(a, b):
    return lax.dot_general(a, b, (((1,), (1,)), ((), ())), preferred_element_type=F32)


def up(value):
    return value.astype(F32)


def kernel(a_hbm, g_hbm, w_hbm, v_hbm, len_ref, out_ref, *scratch):
    scratch = list(scratch)
    av, gv, at, gt, vg, bg, fw, dl, pp, sc, local, ss, rs = scratch[:13]
    del scratch[:13]

    def take(count):
        got = scratch[:count]
        del scratch[:count]
        return got

    wg = take(len(WP))
    ps, pnear, pfar, pz = (take(len(GP)) for _ in range(4))
    gsib, gcore, gown, gs, gnear, gfar, gz = (take(len(GP)) for _ in range(7))
    gpre = take(len(GP))

    f = lax.axis_index("fsdp")
    t = lax.axis_index("tp")
    x, zh, core = f // 4, (f // 2) % 2, f % 2
    zl, y = t // 4, t % 4

    def fid(dx, r, other_core=0):
        c = core if other_core == 0 else 1 - core
        z = zh if r == 0 else 1 - zh
        return ((x + dx) % NX) * 4 + z * 2 + c

    def tid(dy, r):
        z = zl if r == 0 else 1 - zl
        return z * NY + (y + dy) % NY

    z_dev, sib = (fid(0, 1), t), (fid(0, 0, 1), t)
    xp, xm, x2 = (fid(1, 0), t), (fid(3, 0), t), (fid(2, 0), t)
    xps, xms, x2s = (fid(1, 0, 1), t), (fid(3, 0, 1), t), (fid(2, 0, 1), t)
    zl_dev = (f, tid(0, 1))
    yp, ym, y2 = (f, tid(1, 0)), (f, tid(3, 0)), (f, tid(2, 0))
    zd_dev = (fid(0, 1), tid(0, 1))
    peers = (z_dev, sib, xp, xm, x2, xps, xms, x2s, zl_dev, yp, ym, y2, zd_dev)

    def wrows(src):
        return pl.ds(pl.multiple_of(src * WR, 64), WR)

    def vrows(src):
        return pl.ds(pl.multiple_of(src * VR, VR), VR)

    loads = [
        pltpu.make_async_copy(a_hbm, av, local.at[0]),
        pltpu.make_async_copy(g_hbm, gv, local.at[1]),
        pltpu.make_async_copy(v_hbm, vg.at[vrows(f)], local.at[2]),
    ]
    load_w = [
        pltpu.make_async_copy(w_hbm.at[:, pl.ds(first, width)], wg[c].at[wrows(f)], local.at[3 + c])
        for c, (first, width) in enumerate(WP)
    ]
    for load in loads + load_w:
        load.start()

    barrier = pltpu.get_barrier_semaphore()
    for peer in peers:
        pl.semaphore_signal(barrier, inc=1, device_id=peer, device_id_type=MESH)
    pl.semaphore_wait(barrier, len(peers))

    sent, sems, steps = [], {}, {}

    def remote(src, dst, key, dev):
        k = sems.setdefault(key, len(sems))
        return pltpu.make_async_remote_copy(
            src_ref=src, dst_ref=dst, send_sem=ss.at[k], recv_sem=rs.at[k], device_id=dev, device_id_type=MESH
        )

    def send(src, dst, key, dev):
        copy = remote(src, dst, key, dev)
        copy.start()
        sent.append(copy)

    def arrived(dst, key):
        remote(dst, dst, key, sib).wait_recv()

    def step(name, run, *args):
        steps[name] = lambda: run(*args)

    def turn(src, dst, quarter):
        if quarter == 0:
            loads[0 if src is av else 1].wait()
        part = D // 128 // 4

        @pl.loop(quarter * part, (quarter + 1) * part, unroll=2)
        def _(j):
            col = pl.multiple_of(j * 128, 128)
            dst[pl.ds(col, 128), :] = src[:, pl.ds(col, 128)].T

    for quarter in range(4):
        step(f"ta{quarter}", turn, av, at, quarter)
        step(f"tg{quarter}", turn, gv, gt, quarter)

    def gather(n, own, place, load):
        def start():
            dst = place(f)
            send(own, dst, (n, "z"), z_dev)
            send(own, dst, (n, "p", 0), xp)
            send(own, dst, (n, "m", 0), xm)
            send(own, dst, (n, "s", 0, 0), sib)

        def over_z():
            ref = place(fid(0, 1))
            arrived(ref, (n, "z"))
            send(ref, ref, (n, "p", 1), xp)
            send(ref, ref, (n, "m", 1), xm)
            send(ref, ref, (n, "s", 0, 1), sib)

        def behind(r):
            ref = place(fid(3, r))
            arrived(ref, (n, "p", r))
            if r == 0:
                send(ref, ref, (n, "f", 0), xp)
            send(ref, ref, (n, "s", 3, r), sib)

        def ahead(r):
            ref = place(fid(1, r))
            arrived(ref, (n, "m", r))
            if r == 1:
                send(ref, ref, (n, "f", 1), xm)
            send(ref, ref, (n, "s", 1, r), sib)

        def far(r):
            ref = place(fid(2, r))
            arrived(ref, (n, "f", r))
            send(ref, ref, (n, "s", 2, r), sib)

        def end():
            load.wait()
            for dx in range(NX):
                for r in range(2):
                    arrived(place(fid(dx, r, 1)), (n, "s", dx, r))

        step(f"{n}.start", start)
        step(f"{n}.z", over_z)
        for r in range(2):
            step(f"{n}.b{r}", behind, r)
            step(f"{n}.a{r}", ahead, r)
            step(f"{n}.f{r}", far, r)
        step(f"{n}.sib", end)

    def w_place(c):
        return lambda src: wg[c].at[wrows(src)]

    for c, (first, width) in enumerate(WP):
        gather(f"w{c}", w_hbm.at[:, pl.ds(first, width)], w_place(c), load_w[c])
    gather("v0", v_hbm, lambda src: vg.at[vrows(src)], loads[2])

    def keep(j, block):
        row_of = lax.broadcasted_iota(jnp.int32, block.shape, 0)
        return jnp.where(row_of < len_ref[j], block, jnp.zeros_like(block))

    halves = (slice(0, LEN), slice(LEN, ROWS))

    def back(c):
        first, width = WP[c]
        n, route = f"b{c}", ROUTE_B[c]

        def cols(src):
            return pl.ds(pl.multiple_of(src * CT + first, 128), width)

        def block(dy, r):
            return bg.at[:, cols(tid(dy, r))]

        def half(dy, j):
            return bg.at[pl.ds(j * LEN, LEN), cols(tid(dy, 0))]

        def project():
            @pl.loop(0, ROWS // LEN, unroll=2)
            def _(j):
                r0 = pl.ds(pl.multiple_of(j * LEN, LEN), LEN)
                bg[r0, cols(t)] = keep(j, dot(gv[r0, :], wg[c][...]).astype(BF16))

            own = block(0, 0)
            if route == "z":
                send(own, own, (n, "z", 0), zl_dev)
            send(own, own, (n, "p", 0), yp)
            send(own, own, (n, "m", 0), ym)
            if route == "y":
                send(own, own, (n, "z", 0), zl_dev)

        def forward():
            @pl.loop(0, ROWS // LEN, unroll=2)
            def _(j):
                r0 = pl.ds(pl.multiple_of(j * LEN, LEN), LEN)
                fw[r0, first : first + width] = dot(av[r0, :], wg[c][...]).astype(BF16)

        def z_first():
            ref = block(0, 1)
            arrived(ref, (n, "z", 0))
            send(ref, ref, (n, "p", 1), yp)
            send(ref, ref, (n, "m", 1), ym)

        def behind():
            ref = block(3, 0)
            arrived(ref, (n, "p", 0))
            if route == "z":
                send(ref, ref, (n, "f", 0), yp)
            else:
                part = half(3, 0)
                send(part, part, (n, "f", 0), yp)
                send(ref, ref, (n, "z", 3), zl_dev)

        def ahead():
            if route == "z":
                ref = block(1, 1)
                arrived(ref, (n, "m", 1))
                send(ref, ref, (n, "f", 1), ym)
            else:
                ref, part = block(1, 0), half(1, 1)
                arrived(ref, (n, "m", 0))
                send(part, part, (n, "f", 1), ym)
                send(ref, ref, (n, "z", 1), zl_dev)

        def z_last():
            arrived(half(2, 0), (n, "f", 0))
            arrived(half(2, 1), (n, "f", 1))
            ref = block(2, 0)
            send(ref, ref, (n, "z", 2), zl_dev)

        def end():
            if route == "z":
                arrived(block(1, 0), (n, "m", 0))
                arrived(block(3, 1), (n, "p", 1))
                arrived(block(2, 0), (n, "f", 0))
                arrived(block(2, 1), (n, "f", 1))
            else:
                for dy in range(NY):
                    arrived(block(dy, 1), (n, "z", dy))

        step(f"{n}.proj", project)
        step(f"{n}.fwd", forward)
        step(f"{n}.z", z_first if route == "z" else z_last)
        step(f"{n}.yb", behind)
        step(f"{n}.ya", ahead)
        step(f"{n}.end", end)

    for c in range(len(WP)):
        back(c)

    def map_back():
        for first in range(0, CT, 256):
            dl[:, first : first + 256] = dot(bg[...], vg[:, first : first + 256]).astype(BF16)

    step("delta", map_back)

    def ring_sum(n, blocks, near, far, zbuf, plus, minus, across, own, other, finish):
        def start():
            send(blocks.at[4], near.at[0], (n, "pf"), plus)
            send(blocks.at[5], near.at[1], (n, "mf"), minus)
            send(blocks.at[3], far.at[0], (n, "pd"), plus)
            send(blocks.at[6], far.at[1], (n, "md"), minus)

        def through(mine, slot, key, to, out, dev):
            arrived(near.at[slot], (n, key))
            blocks[mine] = (up(blocks[mine]) + up(near[slot])).astype(BF16)
            send(blocks.at[mine], far.at[to], (n, out), dev)

        def end_other():
            arrived(far.at[0], (n, "pd"))
            arrived(far.at[3], (n, "m2"))
            blocks[1] = (up(other()) + up(far[0]) + up(far[3])).astype(BF16)
            send(blocks.at[1], zbuf, (n, "z"), across)

        def last():
            arrived(far.at[1], (n, "md"))
            arrived(far.at[2], (n, "p2"))
            arrived(zbuf, (n, "z"))
            finish((up(own()) + up(far[1])) + (up(far[2]) + up(zbuf[...])))

        step(f"{n}.mp", through, 2, 0, "pf", 2, "p2", plus)
        step(f"{n}.mm", through, 7, 1, "mf", 3, "m2", minus)
        step(f"{n}.eo", end_other)
        step(f"{n}.last", last)
        return start

    def cross_sum(n, blocks, near, far, zin, plus, minus, across, finish):
        def start():
            send(blocks.at[pl.ds(4, 4)], zin, (n, "z"), across)

        def whole(d, rows):
            return up(blocks[d, rows]) + up(zin[d, rows])

        def middle():
            arrived(zin, (n, "z"))
            for j, key, dev in ((0, "pf", plus), (1, "mf", minus)):
                blocks[2, halves[j]] = whole(2, halves[j]).astype(BF16)
                send(blocks.at[2, pl.ds(j * LEN, LEN)], near.at[j], (n, key), dev)

        def through(d, j, key, to, out, dev):
            arrived(near.at[j], (n, key))
            blocks[d, halves[j]] = (whole(d, halves[j]) + up(near[j])).astype(BF16)
            blocks[d, halves[1 - j]] = whole(d, halves[1 - j]).astype(BF16)
            send(blocks.at[d], far.at[to], (n, out), dev)

        def last():
            arrived(far.at[0], (n, "p2"))
            arrived(far.at[1], (n, "m2"))
            finish(whole(0, slice(0, ROWS)) + (up(far[0]) + up(far[1])))

        step(f"{n}.zm", middle)
        step(f"{n}.mp", through, 1, 0, "pf", 0, "p2", plus)
        step(f"{n}.mm", through, 3, 1, "mf", 1, "m2", minus)
        step(f"{n}.last", last)
        return start

    def proxy(s):
        first, width = GP[s]
        n, ring_first = f"p{s}", ROUTE_P[s] == "z"

        def finish(total):
            total = total.astype(BF16)
            for j in range(ROWS // LEN):
                pp[halves[j], first : first + width] = keep(j, total[halves[j]])

        if ring_first:
            start = ring_sum(
                n, ps[s], pnear[s], pfar[s], pz[s], yp, ym, zl_dev, lambda: ps[s][0], lambda: ps[s][1], finish
            )
        else:
            start = cross_sum(n, ps[s], pnear[s], pfar[s], pz[s], yp, ym, zl_dev, finish)

        def partial():
            @pl.loop(0, 2 * NY, unroll=4)
            def _(i):
                dy, r = (i // 2, i % 2) if ring_first else (i % 4, i // 4)
                dest = ((zl + r) % 2) * NY + (y + dy) % NY
                rows = pl.ds(pl.multiple_of(dest * CT + first, 128), width)
                ps[s][i] = dot_t(fw[...], vg[rows, :]).astype(BF16)

        step(f"{n}.part", partial)
        step(f"{n}.go", start)

    def gradient(s):
        first, width = GP[s]
        n, cols = f"g{s}", slice(first, first + width)

        def rows(i, c):
            return wrows(((x + i // 2) % NX) * 4 + ((zh + i % 2) % 2) * 2 + c)

        def term(i, c, had):
            of_out = dot(gt[rows(i, c), :], pp[:, cols])
            if EARLY[s]:
                return had[i] + of_out
            return dot(at[rows(i, c), :], dl[:, cols]) + of_out

        def for_sibling():
            @pl.loop(0, 2 * NX, unroll=4)
            def _(i):
                gsib[s][i] = term(i, 1 - core, gpre[s]).astype(BF16)

            send(gsib[s], gcore[s], (n, "c"), sib)

        def for_own():
            @pl.loop(0, 2 * NX, unroll=4)
            def _(i):
                gown[s][i] = term(i, core, gown[s])

        def finish(total):
            gpre[s][0] = total
            square = jnp.sum((total * total).reshape(WR // 8, 8, width), axis=0)
            square = sum(square[:, k : k + 128] for k in range(0, width, 128))
            sc[0] = square if s == 0 else sc[0] + square

        start = ring_sum(
            n, gs[s], gnear[s], gfar[s], gz[s], xp, xm, z_dev, lambda: gown[s][0], lambda: gown[s][1], finish
        )

        def combine():
            arrived(gcore[s], (n, "c"))

            @pl.loop(0, 2 * NX)
            def _(i):
                whole = gown[s][i] + up(gcore[s][i])
                gown[s][i] = whole
                gs[s][i] = whole.astype(BF16)

            start()

        step(f"{n}.sb", for_sibling)
        step(f"{n}.ow", for_own)
        step(f"{n}.comb", combine)

    def delta_term(h):
        first = GP[2 * h][0]

        @pl.loop(0, 2 * NX, unroll=2)
        def _(i):
            base = ((x + i // 2) % NX) * 4 + ((zh + i % 2) % 2) * 2
            for c, to in ((1 - core, gpre), (core, gown)):
                both = dot(at[wrows(base + c), :], dl[:, first : first + 256])
                to[2 * h][i] = both[:, 0:128]
                to[2 * h + 1][i] = both[:, 128:256]

    for s in range(len(GP)):
        proxy(s)
        gradient(s)
    for h in range(len(GP) // 2):
        step(f"pre{h}", delta_term, h)

    for name in ORDER:
        steps.pop(name)()
    assert not steps

    base = 0
    for devs in ((sib, xp, xm, x2, xps, xms, x2s), (zl_dev, z_dev, zd_dev), (yp, ym, y2)):
        for j, dev in enumerate(devs):
            send(sc.at[base], sc.at[base + 1 + j], ("q", base, j), dev)
        total = sc[base]
        for j in range(len(devs)):
            arrived(sc.at[base + 1 + j], ("q", base, j))
            total = total + sc[base + 1 + j]
        base = base + 1 + len(devs)
        sc[base] = total
    scale = lax.rsqrt(jnp.sum(sc[base]) / (D * PD) + 1e-6)
    for s, (first, width) in enumerate(GP):
        out_ref[:, first : first + width] = (gpre[s][0] * scale).astype(BF16)
    for copy in sent:
        copy.wait_send()
    assert len(sems) <= SEMS


def per_device(activations, cotangent, lengths, grow_operator, proxy_weight):
    anywhere = pl.BlockSpec(memory_space=pl.ANY)

    def for_pieces(rows, shapes, kind=BF16):
        return [pltpu.VMEM(shape + (rows, width), kind) for (_, width), shape in zip(GP, shapes)]

    def same(*shape):
        return [shape] * len(GP)

    def routed(ring, cross):
        return [ring if route == "z" else cross for route in ROUTE_P]

    near = [
        pltpu.VMEM((2, ROWS if route == "z" else LEN, width), BF16) for (_, width), route in zip(GP, ROUTE_P)
    ]
    pre = [
        pltpu.VMEM((2 * NX, WR, width) if early else (8, 128), F32) for (_, width), early in zip(GP, EARLY)
    ]
    return pl.pallas_call(
        kernel,
        out_shape=jax.ShapeDtypeStruct((WR, CT), BF16),
        in_specs=[anywhere] * 4 + [pl.BlockSpec(memory_space=pltpu.SMEM)],
        out_specs=pl.BlockSpec(memory_space=pltpu.VMEM),
        scratch_shapes=[
            pltpu.VMEM((ROWS, D), BF16),
            pltpu.VMEM((ROWS, D), BF16),
            pltpu.VMEM((D, ROWS), BF16),
            pltpu.VMEM((D, ROWS), BF16),
            pltpu.VMEM((PD, CT), BF16),
            pltpu.VMEM((ROWS, PD), BF16),
            pltpu.VMEM((ROWS, CT), BF16),
            pltpu.VMEM((ROWS, CT), BF16),
            pltpu.VMEM((ROWS, CT), BF16),
            pltpu.VMEM((17, 8, 128), F32),
            pltpu.SemaphoreType.DMA((3 + len(WP),)),
            pltpu.SemaphoreType.DMA((SEMS,)),
            pltpu.SemaphoreType.DMA((SEMS,)),
        ]
        + [pltpu.VMEM((D, width), BF16) for _, width in WP]
        + for_pieces(ROWS, same(2 * NY))
        + near
        + for_pieces(ROWS, routed((4,), (2,)))
        + for_pieces(ROWS, routed((), (4,)))
        + for_pieces(WR, same(2 * NX))
        + for_pieces(WR, same(2 * NX))
        + for_pieces(WR, same(2 * NX), F32)
        + for_pieces(WR, same(2 * NX))
        + for_pieces(WR, same(2))
        + for_pieces(WR, same(4))
        + for_pieces(WR, same())
        + pre,
        compiler_params=pltpu.CompilerParams(
            collective_id=0, has_side_effects=True, vmem_limit_bytes=VMEM_BYTES
        ),
    )(activations, cotangent, grow_operator, proxy_weight, lengths)


def solution(mesh):
    placed = (P("fsdp", None), P("fsdp", None), P("fsdp"), P("fsdp", "tp"), P("fsdp", "tp"))
    return jax.shard_map(
        per_device, mesh=mesh, in_specs=placed, out_specs=P("fsdp", "tp"), check_vma=False
    )
```

```python
import jax
import jax.numpy as jnp
from jax import lax
from jax.experimental import pallas as pl
from jax.experimental.pallas import tpu as pltpu
from jax.sharding import PartitionSpec as P

MESH = pl.DeviceIdType.MESH
F32, BF16 = jnp.float32, jnp.bfloat16

D = 5120
PD = 4096
LEN = 256
ROWS = 512
WR = 320
VR = 256
CT = 512
NX = 4
NY = 4

WP = ((0, 128), (128, 128), (256, 256))
GP = ((0, 128), (128, 128), (256, 128), (384, 128))
ROUTE_B = "zzy"
ROUTE_P = "zzzy"
EARLY = (1, 1, 1, 1)
SEMS = 192

ORDER = (
    "w0.start", "w2.start", "w0.z", "w1.start", "w2.z", "w0.b0", "ta0", "w2.b0",
    "w0.b1", "w1.z", "ta1", "ta2", "ta3", "w2.a0", "w0.a1", "tg0",
    "tg1", "w0.a0", "w2.a1", "tg2", "w2.b1", "w1.b0", "w1.a1", "w1.a0",
    "w0.f0", "v0.start", "w0.f1", "w0.sib", "w2.f0", "b0.proj", "w2.f1", "w2.sib",
    "b2.proj", "tg3", "w1.b1", "v0.z", "b0.fwd", "b0.z", "w1.f0", "w1.f1",
    "v0.a0", "w1.sib", "b1.proj", "b2.ya", "v0.b0", "b2.yb", "v0.b1", "v0.a1",
    "b1.z", "b0.yb", "b2.fwd", "b1.fwd", "b1.yb", "b2.z", "b0.ya", "v0.f0",
    "v0.f1", "v0.sib", "b1.ya", "p0.part", "p0.go", "b0.end", "p1.part", "p3.part",
    "p3.go", "p0.mm", "p0.mp", "p1.go", "b2.end", "b1.end", "delta", "p2.part",
    "pre0", "p1.mm", "p0.eo", "p1.mp", "p2.go", "pre1", "p1.eo", "p0.last",
    "g0.sb", "p2.mm", "p2.mp", "g0.ow", "g0.comb", "p3.zm", "p1.last", "g1.sb",
    "p2.eo", "g1.ow", "g1.comb", "p3.mp", "g0.mm", "p3.mm", "g0.mp", "p2.last",
    "g2.sb", "g1.mm", "g2.ow", "p3.last", "g2.comb", "g3.sb", "g3.ow", "g3.comb",
    "g0.eo", "g1.mp", "g2.mm", "g2.mp", "g3.mm", "g1.eo", "g2.eo", "g3.mp",
    "g3.eo", "g0.last", "g1.last", "g2.last", "g3.last",
)
LOAD_AT = "w0.z"
VMEM_BYTES = 63 * 1024 * 1024


def dot(a, b):
    return jnp.dot(a, b, preferred_element_type=F32)


def dot_t(a, b):
    return lax.dot_general(a, b, (((1,), (1,)), ((), ())), preferred_element_type=F32)


def up(value):
    return value.astype(F32)


def kernel(a_hbm, g_hbm, w_hbm, v_hbm, len_ref, out_ref, *scratch):
    scratch = list(scratch)
    av, gv, at, gt, vg, bg, fw, dl, pp, sc, local, ss, rs = scratch[:13]
    del scratch[:13]

    def take(count):
        got = scratch[:count]
        del scratch[:count]
        return got

    wg = take(len(WP))
    ps, pnear, pfar, pz = (take(len(GP)) for _ in range(4))
    gsib, gcore, gown, gs, gnear, gfar, gz = (take(len(GP)) for _ in range(7))
    gpre = take(len(GP))

    f = lax.axis_index("fsdp")
    t = lax.axis_index("tp")
    x, zh, core = f // 4, (f // 2) % 2, f % 2
    zl, y = t // 4, t % 4

    def fid(dx, r, other_core=0):
        c = core if other_core == 0 else 1 - core
        z = zh if r == 0 else 1 - zh
        return ((x + dx) % NX) * 4 + z * 2 + c

    def tid(dy, r):
        z = zl if r == 0 else 1 - zl
        return z * NY + (y + dy) % NY

    z_dev, sib = (fid(0, 1), t), (fid(0, 0, 1), t)
    xp, xm, x2 = (fid(1, 0), t), (fid(3, 0), t), (fid(2, 0), t)
    xps, xms, x2s = (fid(1, 0, 1), t), (fid(3, 0, 1), t), (fid(2, 0, 1), t)
    zl_dev = (f, tid(0, 1))
    yp, ym, y2 = (f, tid(1, 0)), (f, tid(3, 0)), (f, tid(2, 0))
    zd_dev = (fid(0, 1), tid(0, 1))
    peers = (z_dev, sib, xp, xm, x2, xps, xms, x2s, zl_dev, yp, ym, y2, zd_dev)

    def wrows(src):
        return pl.ds(pl.multiple_of(src * WR, 64), WR)

    def vrows(src):
        return pl.ds(pl.multiple_of(src * VR, VR), VR)

    loads = [
        pltpu.make_async_copy(a_hbm, av, local.at[0]),
        pltpu.make_async_copy(g_hbm, gv, local.at[1]),
        pltpu.make_async_copy(v_hbm, vg.at[vrows(f)], local.at[2]),
    ]
    load_w = [
        pltpu.make_async_copy(w_hbm.at[:, pl.ds(first, width)], wg[c].at[wrows(f)], local.at[3 + c])
        for c, (first, width) in enumerate(WP)
    ]

    barrier = pltpu.get_barrier_semaphore()
    for peer in peers:
        pl.semaphore_signal(barrier, inc=1, device_id=peer, device_id_type=MESH)
    pl.semaphore_wait(barrier, len(peers))

    sent, sems, steps = [], {}, {}

    def remote(src, dst, key, dev):
        k = sems.setdefault(key, len(sems))
        return pltpu.make_async_remote_copy(
            src_ref=src, dst_ref=dst, send_sem=ss.at[k], recv_sem=rs.at[k], device_id=dev, device_id_type=MESH
        )

    def send(src, dst, key, dev):
        copy = remote(src, dst, key, dev)
        copy.start()
        sent.append(copy)

    def arrived(dst, key):
        remote(dst, dst, key, sib).wait_recv()

    def step(name, run, *args):
        steps[name] = lambda: run(*args)

    def turn(src, dst, quarter):
        if quarter == 0:
            loads[0 if src is av else 1].wait()
        part = D // 128 // 4

        @pl.loop(quarter * part, (quarter + 1) * part, unroll=2)
        def _(j):
            col = pl.multiple_of(j * 128, 128)
            dst[pl.ds(col, 128), :] = src[:, pl.ds(col, 128)].T

    for quarter in range(4):
        step(f"ta{quarter}", turn, av, at, quarter)
        step(f"tg{quarter}", turn, gv, gt, quarter)

    def gather(n, own, place, load):
        def start():
            dst = place(f)
            send(own, dst, (n, "z"), z_dev)
            send(own, dst, (n, "p", 0), xp)
            send(own, dst, (n, "m", 0), xm)
            send(own, dst, (n, "s", 0, 0), sib)

        def over_z():
            ref = place(fid(0, 1))
            arrived(ref, (n, "z"))
            send(ref, ref, (n, "p", 1), xp)
            send(ref, ref, (n, "m", 1), xm)
            send(ref, ref, (n, "s", 0, 1), sib)

        def behind(r):
            ref = place(fid(3, r))
            arrived(ref, (n, "p", r))
            if r == 0:
                send(ref, ref, (n, "f", 0), xp)
            send(ref, ref, (n, "s", 3, r), sib)

        def ahead(r):
            ref = place(fid(1, r))
            arrived(ref, (n, "m", r))
            if r == 1:
                send(ref, ref, (n, "f", 1), xm)
            send(ref, ref, (n, "s", 1, r), sib)

        def far(r):
            ref = place(fid(2, r))
            arrived(ref, (n, "f", r))
            send(ref, ref, (n, "s", 2, r), sib)

        def end():
            load.wait()
            for dx in range(NX):
                for r in range(2):
                    arrived(place(fid(dx, r, 1)), (n, "s", dx, r))

        step(f"{n}.start", start)
        step(f"{n}.z", over_z)
        for r in range(2):
            step(f"{n}.b{r}", behind, r)
            step(f"{n}.a{r}", ahead, r)
            step(f"{n}.f{r}", far, r)
        step(f"{n}.sib", end)

    def w_place(c):
        return lambda src: wg[c].at[wrows(src)]

    for c, (first, width) in enumerate(WP):
        gather(f"w{c}", w_hbm.at[:, pl.ds(first, width)], w_place(c), load_w[c])
    gather("v0", v_hbm, lambda src: vg.at[vrows(src)], loads[2])

    def keep(j, block):
        row_of = lax.broadcasted_iota(jnp.int32, block.shape, 0)
        return jnp.where(row_of < len_ref[j], block, jnp.zeros_like(block))

    halves = (slice(0, LEN), slice(LEN, ROWS))

    def back(c):
        first, width = WP[c]
        n, route = f"b{c}", ROUTE_B[c]

        def cols(src):
            return pl.ds(pl.multiple_of(src * CT + first, 128), width)

        def block(dy, r):
            return bg.at[:, cols(tid(dy, r))]

        def half(dy, j):
            return bg.at[pl.ds(j * LEN, LEN), cols(tid(dy, 0))]

        def project():
            @pl.loop(0, ROWS // LEN, unroll=2)
            def _(j):
                r0 = pl.ds(pl.multiple_of(j * LEN, LEN), LEN)
                bg[r0, cols(t)] = keep(j, dot(gv[r0, :], wg[c][...]).astype(BF16))

            own = block(0, 0)
            if route == "z":
                send(own, own, (n, "z", 0), zl_dev)
            send(own, own, (n, "p", 0), yp)
            send(own, own, (n, "m", 0), ym)
            if route == "y":
                send(own, own, (n, "z", 0), zl_dev)

        def forward():
            @pl.loop(0, ROWS // LEN, unroll=2)
            def _(j):
                r0 = pl.ds(pl.multiple_of(j * LEN, LEN), LEN)
                fw[r0, first : first + width] = dot(av[r0, :], wg[c][...]).astype(BF16)

        def z_first():
            ref = block(0, 1)
            arrived(ref, (n, "z", 0))
            send(ref, ref, (n, "p", 1), yp)
            send(ref, ref, (n, "m", 1), ym)

        def behind():
            ref = block(3, 0)
            arrived(ref, (n, "p", 0))
            if route == "z":
                send(ref, ref, (n, "f", 0), yp)
            else:
                part = half(3, 0)
                send(part, part, (n, "f", 0), yp)
                send(ref, ref, (n, "z", 3), zl_dev)

        def ahead():
            if route == "z":
                ref = block(1, 1)
                arrived(ref, (n, "m", 1))
                send(ref, ref, (n, "f", 1), ym)
            else:
                ref, part = block(1, 0), half(1, 1)
                arrived(ref, (n, "m", 0))
                send(part, part, (n, "f", 1), ym)
                send(ref, ref, (n, "z", 1), zl_dev)

        def z_last():
            arrived(half(2, 0), (n, "f", 0))
            arrived(half(2, 1), (n, "f", 1))
            ref = block(2, 0)
            send(ref, ref, (n, "z", 2), zl_dev)

        def end():
            if route == "z":
                arrived(block(1, 0), (n, "m", 0))
                arrived(block(3, 1), (n, "p", 1))
                arrived(block(2, 0), (n, "f", 0))
                arrived(block(2, 1), (n, "f", 1))
            else:
                for dy in range(NY):
                    arrived(block(dy, 1), (n, "z", dy))

        step(f"{n}.proj", project)
        step(f"{n}.fwd", forward)
        step(f"{n}.z", z_first if route == "z" else z_last)
        step(f"{n}.yb", behind)
        step(f"{n}.ya", ahead)
        step(f"{n}.end", end)

    for c in range(len(WP)):
        back(c)

    def map_back():
        for first in range(0, CT, 256):
            dl[:, first : first + 256] = dot(bg[...], vg[:, first : first + 256]).astype(BF16)

    step("delta", map_back)

    def ring_sum(n, blocks, near, far, zbuf, plus, minus, across, own, other, finish):
        def start():
            send(blocks.at[4], near.at[0], (n, "pf"), plus)
            send(blocks.at[5], near.at[1], (n, "mf"), minus)
            send(blocks.at[3], far.at[0], (n, "pd"), plus)
            send(blocks.at[6], far.at[1], (n, "md"), minus)

        def through(mine, slot, key, to, out, dev):
            arrived(near.at[slot], (n, key))
            blocks[mine] = (up(blocks[mine]) + up(near[slot])).astype(BF16)
            send(blocks.at[mine], far.at[to], (n, out), dev)

        def end_other():
            arrived(far.at[0], (n, "pd"))
            arrived(far.at[3], (n, "m2"))
            blocks[1] = (up(other()) + up(far[0]) + up(far[3])).astype(BF16)
            send(blocks.at[1], zbuf, (n, "z"), across)

        def last():
            arrived(far.at[1], (n, "md"))
            arrived(far.at[2], (n, "p2"))
            arrived(zbuf, (n, "z"))
            finish((up(own()) + up(far[1])) + (up(far[2]) + up(zbuf[...])))

        step(f"{n}.mp", through, 2, 0, "pf", 2, "p2", plus)
        step(f"{n}.mm", through, 7, 1, "mf", 3, "m2", minus)
        step(f"{n}.eo", end_other)
        step(f"{n}.last", last)
        return start

    def cross_sum(n, blocks, near, far, zin, plus, minus, across, finish):
        def start():
            send(blocks.at[pl.ds(4, 4)], zin, (n, "z"), across)

        def whole(d, rows):
            return up(blocks[d, rows]) + up(zin[d, rows])

        def middle():
            arrived(zin, (n, "z"))
            for j, key, dev in ((0, "pf", plus), (1, "mf", minus)):
                blocks[2, halves[j]] = whole(2, halves[j]).astype(BF16)
                send(blocks.at[2, pl.ds(j * LEN, LEN)], near.at[j], (n, key), dev)

        def through(d, j, key, to, out, dev):
            arrived(near.at[j], (n, key))
            blocks[d, halves[j]] = (whole(d, halves[j]) + up(near[j])).astype(BF16)
            blocks[d, halves[1 - j]] = whole(d, halves[1 - j]).astype(BF16)
            send(blocks.at[d], far.at[to], (n, out), dev)

        def last():
            arrived(far.at[0], (n, "p2"))
            arrived(far.at[1], (n, "m2"))
            finish(whole(0, slice(0, ROWS)) + (up(far[0]) + up(far[1])))

        step(f"{n}.zm", middle)
        step(f"{n}.mp", through, 1, 0, "pf", 0, "p2", plus)
        step(f"{n}.mm", through, 3, 1, "mf", 1, "m2", minus)
        step(f"{n}.last", last)
        return start

    def proxy(s):
        first, width = GP[s]
        n, ring_first = f"p{s}", ROUTE_P[s] == "z"

        def finish(total):
            total = total.astype(BF16)
            for j in range(ROWS // LEN):
                pp[halves[j], first : first + width] = keep(j, total[halves[j]])

        if ring_first:
            start = ring_sum(
                n, ps[s], pnear[s], pfar[s], pz[s], yp, ym, zl_dev, lambda: ps[s][0], lambda: ps[s][1], finish
            )
        else:
            start = cross_sum(n, ps[s], pnear[s], pfar[s], pz[s], yp, ym, zl_dev, finish)

        def partial():
            @pl.loop(0, 2 * NY, unroll=4)
            def _(i):
                dy, r = (i // 2, i % 2) if ring_first else (i % 4, i // 4)
                dest = ((zl + r) % 2) * NY + (y + dy) % NY
                rows = pl.ds(pl.multiple_of(dest * CT + first, 128), width)
                ps[s][i] = dot_t(fw[...], vg[rows, :]).astype(BF16)

        step(f"{n}.part", partial)
        step(f"{n}.go", start)

    def gradient(s):
        first, width = GP[s]
        n, cols = f"g{s}", slice(first, first + width)

        def rows(i, c):
            return wrows(((x + i // 2) % NX) * 4 + ((zh + i % 2) % 2) * 2 + c)

        def term(i, c, had):
            of_out = dot(gt[rows(i, c), :], pp[:, cols])
            if EARLY[s]:
                return had[i] + of_out
            return dot(at[rows(i, c), :], dl[:, cols]) + of_out

        def for_sibling():
            @pl.loop(0, 2 * NX, unroll=4)
            def _(i):
                gsib[s][i] = term(i, 1 - core, gpre[s]).astype(BF16)

            send(gsib[s], gcore[s], (n, "c"), sib)

        def for_own():
            @pl.loop(0, 2 * NX, unroll=4)
            def _(i):
                gown[s][i] = term(i, core, gown[s])

        def finish(total):
            gpre[s][0] = total
            square = jnp.sum((total * total).reshape(WR // 8, 8, width), axis=0)
            square = sum(square[:, k : k + 128] for k in range(0, width, 128))
            sc[0] = square if s == 0 else sc[0] + square

        start = ring_sum(
            n, gs[s], gnear[s], gfar[s], gz[s], xp, xm, z_dev, lambda: gown[s][0], lambda: gown[s][1], finish
        )

        def combine():
            arrived(gcore[s], (n, "c"))

            @pl.loop(0, 2 * NX)
            def _(i):
                whole = gown[s][i] + up(gcore[s][i])
                gown[s][i] = whole
                gs[s][i] = whole.astype(BF16)

            start()

        step(f"{n}.sb", for_sibling)
        step(f"{n}.ow", for_own)
        step(f"{n}.comb", combine)

    def delta_term(h):
        first = GP[2 * h][0]

        @pl.loop(0, 2 * NX, unroll=2)
        def _(i):
            base = ((x + i // 2) % NX) * 4 + ((zh + i % 2) % 2) * 2
            for c, to in ((1 - core, gpre), (core, gown)):
                both = dot(at[wrows(base + c), :], dl[:, first : first + 256])
                to[2 * h][i] = both[:, 0:128]
                to[2 * h + 1][i] = both[:, 128:256]

    for s in range(len(GP)):
        proxy(s)
        gradient(s)
    for h in range(len(GP) // 2):
        step(f"pre{h}", delta_term, h)

    for name in ORDER:
        if name == LOAD_AT:
            for load in loads + load_w:
                load.start()
        steps.pop(name)()
    assert not steps

    base = 0
    for devs in ((sib, xp, xm, x2, xps, xms, x2s), (zl_dev, z_dev, zd_dev), (yp, ym, y2)):
        for j, dev in enumerate(devs):
            send(sc.at[base], sc.at[base + 1 + j], ("q", base, j), dev)
        total = sc[base]
        for j in range(len(devs)):
            arrived(sc.at[base + 1 + j], ("q", base, j))
            total = total + sc[base + 1 + j]
        base = base + 1 + len(devs)
        sc[base] = total
    scale = lax.rsqrt(jnp.sum(sc[base]) / (D * PD) + 1e-6)
    for s, (first, width) in enumerate(GP):
        out_ref[:, first : first + width] = (gpre[s][0] * scale).astype(BF16)
    for copy in sent:
        copy.wait_send()
    assert len(sems) <= SEMS


def per_device(activations, cotangent, lengths, grow_operator, proxy_weight):
    anywhere = pl.BlockSpec(memory_space=pl.ANY)

    def for_pieces(rows, shapes, kind=BF16):
        return [pltpu.VMEM(shape + (rows, width), kind) for (_, width), shape in zip(GP, shapes)]

    def same(*shape):
        return [shape] * len(GP)

    def routed(ring, cross):
        return [ring if route == "z" else cross for route in ROUTE_P]

    near = [
        pltpu.VMEM((2, ROWS if route == "z" else LEN, width), BF16) for (_, width), route in zip(GP, ROUTE_P)
    ]
    pre = [
        pltpu.VMEM((2 * NX, WR, width) if early else (8, 128), F32) for (_, width), early in zip(GP, EARLY)
    ]
    return pl.pallas_call(
        kernel,
        out_shape=jax.ShapeDtypeStruct((WR, CT), BF16),
        in_specs=[anywhere] * 4 + [pl.BlockSpec(memory_space=pltpu.SMEM)],
        out_specs=pl.BlockSpec(memory_space=pltpu.VMEM),
        scratch_shapes=[
            pltpu.VMEM((ROWS, D), BF16),
            pltpu.VMEM((ROWS, D), BF16),
            pltpu.VMEM((D, ROWS), BF16),
            pltpu.VMEM((D, ROWS), BF16),
            pltpu.VMEM((PD, CT), BF16),
            pltpu.VMEM((ROWS, PD), BF16),
            pltpu.VMEM((ROWS, CT), BF16),
            pltpu.VMEM((ROWS, CT), BF16),
            pltpu.VMEM((ROWS, CT), BF16),
            pltpu.VMEM((17, 8, 128), F32),
            pltpu.SemaphoreType.DMA((3 + len(WP),)),
            pltpu.SemaphoreType.DMA((SEMS,)),
            pltpu.SemaphoreType.DMA((SEMS,)),
        ]
        + [pltpu.VMEM((D, width), BF16) for _, width in WP]
        + for_pieces(ROWS, same(2 * NY))
        + near
        + for_pieces(ROWS, routed((4,), (2,)))
        + for_pieces(ROWS, routed((), (4,)))
        + for_pieces(WR, same(2 * NX))
        + for_pieces(WR, same(2 * NX))
        + for_pieces(WR, same(2 * NX), F32)
        + for_pieces(WR, same(2 * NX))
        + for_pieces(WR, same(2))
        + for_pieces(WR, same(4))
        + for_pieces(WR, same())
        + pre,
        compiler_params=pltpu.CompilerParams(
            collective_id=0, has_side_effects=True, vmem_limit_bytes=VMEM_BYTES
        ),
    )(activations, cotangent, grow_operator, proxy_weight, lengths)


def solution(mesh):
    placed = (P("fsdp", None), P("fsdp", None), P("fsdp"), P("fsdp", "tp"), P("fsdp", "tp"))
    return jax.shard_map(
        per_device, mesh=mesh, in_specs=placed, out_specs=P("fsdp", "tp"), check_vma=False
    )
```
